32 devices in a mesh: groups: 2 (over y), seq: 4 (over z), row: 2 (over x), col: 2 (over core).
Axes of the slice: x: 2, y: 2, z: 4, core: 2. Of those that a mesh axis runs over, the one named last changes fastest.
Arguments:
- acts: bfloat16 [3072, 4096], P(('groups', 'seq', 'row'), 'col'), parts along dimension 0, may hold values from -9 to 9
- w_query: bfloat16 [4096, 2048], P('seq', ('row', 'col')), may hold values from -0.1875 to 0.1875
- w_key: bfloat16 [4096, 2048], P('seq', ('row', 'col')), may hold values from -0.1875 to 0.1875
- w_value: bfloat16 [4096, 2048], P('seq', ('row', 'col')), may hold values from -0.09375 to 0.09375
Outputs:
- attended: bfloat16 [3072, 2048], P(('groups', 'seq'), ('row', 'col')), parts along dimension 0
The draws below stay inside these ranges and needn't reach their ends.
There are 2 independent parts, one for each index of `groups`. The reference program is written for one: setup_inputs(seed, part) draws one part's arguments, and reference() takes and returns one part's arrays. A program takes and returns all parts, laid end to end along the dimension named above; an argument that names none is the same for every part. Nothing has to cross between parts.
All inputs are finite; a program needn't handle non-finite values.
Results may differ from the reference program's by a relative error of at most 0.0055.
The reference program's roundings to bfloat16 on the way count: a program that leaves them out, or rounds other values in their place, can miss the bound.
Values may be sent and summed in bfloat16 or wider, within the bound.
A program may use at most 64 MiB of HBM per device.

```python
import jax
import jax.numpy as jnp
from jax import lax

D = 4096
HEADS = 16
HD = 128
SPAN = 4
BLOCK = 384
TOKENS = 1536
N_SEQ = 4


def draw_acts(key, part):
    base_key = jax.random.fold_in(key, 0)
    values = jnp.clip(jax.random.normal(base_key, (TOKENS, D), jnp.float32), -6.0, 6.0)
    return values.astype(jnp.bfloat16)


def steps_of(rng, shape, pieces, smallest, high):
    gain = 1.0
    for axis_at, parts in pieces:
        steps = jax.random.uniform(jax.random.fold_in(jax.random.fold_in(rng, 6), axis_at), (parts,), jnp.float32, smallest / len(pieces), high / len(pieces))
        gain = gain * jnp.repeat(jnp.exp(steps), shape[axis_at] // parts).reshape((-1,) + (1,) * (len(shape) - 1 - axis_at))
    return gain


def gaussian(rng, shape, deviation, most, cuts=(), dtype=jnp.bfloat16):
    entries = deviation * jax.random.normal(rng, shape, jnp.float32)
    if cuts:
        entries = entries * steps_of(rng, shape, cuts, -0.22, 0.18)
    return jnp.clip(entries, -most, most).astype(dtype)


def setup_inputs(seed: int = 0, part: int = 0) -> dict:
    arg_keys = jax.random.split(jax.random.key(seed), 5)
    part_splits = jax.random.split(jax.random.fold_in(arg_keys[4], part), 5)
    acts = draw_acts(jax.random.fold_in(jax.random.fold_in(arg_keys[4], part), 71), part)
    w_query = gaussian(arg_keys[1], (D, HEADS * HD), (D // 4) ** -0.5, 0.1875, ((0, 4), (1, 4)))
    w_key = gaussian(arg_keys[2], (D, HEADS * HD), (D // 4) ** -0.5, 0.1875, ((0, 4), (1, 4)))
    w_value = gaussian(arg_keys[3], (D, HEADS * HD), D ** -0.5, 0.09375, ((0, 4), (1, 4)))
    return {"acts": acts, "w_query": w_query, "w_key": w_key, "w_value": w_value}


def reference(acts, w_query, w_key, w_value):
    inputs = acts.astype(jnp.float32)
    width = HEADS * HD

    def project(weight):
        product = jnp.dot(inputs, weight.astype(jnp.float32), precision=lax.Precision.HIGHEST)
        return product.astype(jnp.bfloat16).reshape(N_SEQ, BLOCK, HEADS, HD)
    query = project(w_query)
    keys = project(w_key)
    values = project(w_value)
    scale = 1.0 / jnp.sqrt(jnp.float32(HD))
    offsets = jnp.arange(SPAN).astype(jnp.int32)

    def one_block(index):
        picks = (index - offsets) % N_SEQ
        block_query = query[index].astype(jnp.float32)
        block_keys = keys[picks].reshape(SPAN * BLOCK, HEADS, HD).astype(jnp.float32)
        block_values = values[picks].reshape(SPAN * BLOCK, HEADS, HD).astype(jnp.float32)
        scores = jnp.einsum('qhd,khd->hqk', block_query, block_keys, precision=lax.Precision.HIGHEST) * scale
        top = lax.optimization_barrier(jnp.max(scores, axis=-1, keepdims=True))
        expos = jnp.exp(scores - top)
        total = lax.optimization_barrier(jnp.sum(expos, axis=-1))
        rounded = lax.optimization_barrier(expos.astype(jnp.bfloat16)).astype(jnp.float32)
        summed = jnp.einsum('hqk,khd->qhd', rounded, block_values, precision=lax.Precision.HIGHEST)
        return (summed / jnp.transpose(total)[:, :, None]).astype(jnp.bfloat16)
    result = lax.map(one_block, jnp.arange(N_SEQ).astype(jnp.int32))
    return result.reshape(TOKENS, width)
```

```python
import functools

import jax
import jax.numpy as jnp
from jax import lax
from jax.experimental import pallas as pl
from jax.experimental.pallas import tpu as pltpu
from jax.sharding import PartitionSpec as P

HD = 128
SPAN = 4
CHUNKS = 4
MESH = pl.DeviceIdType.MESH


def head_kernel(
    n, acts, w_query, w_key, w_value, out,
    x_all, w_all, qkv, heads_out,
    local_sem, w_send, w_recv, y_send, y_recv,
    up_send, down_send, z_recv, x_send, x_recv, c_send, c_recv, o_send, o_recv,
):
    g, s = lax.axis_index("groups"), lax.axis_index("seq")
    r, c = lax.axis_index("row"), lax.axis_index("col")
    weights = (w_query, w_key, w_value)
    rows, half_width = acts.shape
    depth = w_query.shape[0]
    half = depth // 2
    block = 2 * rows
    part = rows // CHUNKS

    barrier = pltpu.get_barrier_semaphore()
    for j in range(1, n):
        pl.semaphore_signal(barrier, inc=1, device_id={"seq": lax.rem(s + j, n)}, device_id_type=MESH)
    pl.semaphore_signal(barrier, inc=1, device_id={"groups": 1 - g}, device_id_type=MESH)
    pl.semaphore_signal(barrier, inc=1, device_id={"row": 1 - r}, device_id_type=MESH)
    pl.semaphore_signal(barrier, inc=1, device_id={"col": 1 - c}, device_id_type=MESH)
    pl.semaphore_wait(barrier, n + 2)

    def remote(src, dst, send, recv, **device):
        return pltpu.make_async_remote_copy(
            src_ref=src, dst_ref=dst, send_sem=send, recv_sem=recv, device_id=device, device_id_type=MESH
        )

    def w_rows(owner, which):
        return pl.ds(pl.multiple_of(owner * depth + which * half, half), half)

    def w_copy(j, i):
        dest = lax.rem(s + j, n)
        return remote(
            weights[i].at[pl.ds(pl.multiple_of(g * half, half), half), pl.ds(pl.multiple_of(dest * HD, HD), HD)],
            w_all.at[w_rows(s, g), pl.ds(i * HD, HD)],
            w_send.at[j - 1, i], w_recv.at[j - 1, i], seq=dest,
        )

    def w_arrival(j, i):
        owner = lax.rem(s + n - j, n)
        here = w_all.at[w_rows(owner, g), pl.ds(i * HD, HD)]
        return remote(here, here, w_send.at[j - 1, i], w_recv.at[j - 1, i], seq=lax.rem(s + j, n))

    def y_copy(j):
        owner = lax.rem(s + n - j, n)
        here = w_all.at[w_rows(owner, g), :]
        return remote(here, here, y_send.at[j - 1], y_recv.at[j - 1], groups=1 - g)

    def y_arrival(j):
        owner = lax.rem(s + n - j, n)
        here = w_all.at[w_rows(owner, 1 - g), :]
        return remote(here, here, y_send.at[j - 1], y_recv.at[j - 1], groups=1 - g)

    def spot(b, rr, cc, k):
        return x_all.at[b, cc, pl.ds(pl.multiple_of(rr * rows + k * part, part), part), :]

    def source(b, k, own):
        return acts.at[pl.ds(pl.multiple_of(k * part, part), part), :] if own else spot(b, r, c, k)

    def up_copy(b, k, own=False):
        return remote(source(b, k, own), spot(b, r, c, k), up_send.at[b, k], z_recv.at[b, k], seq=s + 1)

    def down_copy(b, k, own=False):
        return remote(source(b, k, own), spot(b, r, c, k), down_send.at[b, k], z_recv.at[b, k], seq=s - 1)

    def x_copy(b, k, own=False):
        return remote(source(b, k, own), spot(b, r, c, k), x_send.at[b, k], x_recv.at[b, k], row=1 - r)

    def x_arrival(b, k):
        here = spot(b, 1 - r, c, k)
        return remote(here, here, x_send.at[b, k], x_recv.at[b, k], row=1 - r)

    def c_copy(b, k, rr, own=False):
        src = source(b, k, True) if own else spot(b, rr, c, k)
        return remote(src, spot(b, rr, c, k), c_send.at[rr, b, k], c_recv.at[rr, b, k], col=1 - c)

    def c_arrival(b, k, rr):
        here = spot(b, rr, 1 - c, k)
        return remote(here, here, c_send.at[rr, b, k], c_recv.at[rr, b, k], col=1 - c)

    for j in range(1, n):
        for i in range(3):
            w_copy(j, i).start()

    @pl.loop(0, CHUNKS)
    def _(k):
        @pl.when(s < n - 1)
        def _():
            up_copy(s, k, True).start()

        @pl.when(s > 0)
        def _():
            down_copy(s, k, True).start()

        x_copy(s, k, True).start()
        c_copy(s, k, r, True).start()

    own_copies = [
        pltpu.make_async_copy(
            acts, x_all.at[s, c, pl.ds(pl.multiple_of(r * rows, rows), rows), :], local_sem.at[0]
        )
    ] + [
        pltpu.make_async_copy(
            weights[i].at[:, pl.ds(pl.multiple_of(s * HD, HD), HD)],
            w_all.at[pl.ds(pl.multiple_of(s * depth, depth), depth), pl.ds(i * HD, HD)],
            local_sem.at[1 + i],
        )
        for i in range(3)
    ]
    for copy in own_copies:
        copy.start()

    def each_at(t, body):
        if t == 0:
            body(s, 0)
            return
        pl.when(s - t >= 0)(lambda: body(s - t, 1))
        pl.when(s + t < n)(lambda: body(s + t, -1))

    def pass_on(b, side, k):
        here = spot(b, r, c, k)
        remote(here, here, up_send.at[b, k], z_recv.at[b, k], row=1 - r).wait_recv()
        if side > 0:
            pl.when(s < n - 1)(lambda: up_copy(b, k).start())
        else:
            pl.when(s > 0)(lambda: down_copy(b, k).start())
        x_copy(b, k).start()
        c_copy(b, k, r).start()

    def across(b, k):
        x_arrival(b, k).wait_recv()
        c_copy(b, k, 1 - r).start()

    def project(b):
        @pl.loop(0, CHUNKS)
        def _(k):
            c_arrival(b, k, 0).wait_recv()
            c_arrival(b, k, 1).wait_recv()

        total = jnp.dot(x_all[b, 0], w_all[:half_width, :], preferred_element_type=jnp.float32)
        total += jnp.dot(x_all[b, 1], w_all[half_width:, :], preferred_element_type=jnp.float32)
        qkv[pl.ds(pl.multiple_of(b * block, block), block), :] = total.astype(jnp.bfloat16)

    for t in range(1, n):
        @pl.loop(0, CHUNKS)
        def _(k):
            each_at(t, lambda b, side: pass_on(b, side, k))
            each_at(t - 1, lambda b, side: across(b, k))

        if t == 1:
            for j in range(1, n):
                for i in range(3):
                    w_arrival(j, i).wait_recv()
                y_copy(j).start()
        if t == n - 2:
            for copy in own_copies:
                copy.wait()
            for j in range(1, n):
                y_arrival(j).wait_recv()
            first, last = jnp.maximum(s - (n - 3), 0), jnp.minimum(s + (n - 3), n - 1)
            pl.loop(first, last + 1)(project)
        if t == n - 1:
            each_at(n - 2, lambda b, side: project(b))

    @pl.loop(0, CHUNKS)
    def _(k):
        each_at(n - 1, lambda b, side: across(b, k))

    each_at(n - 1, lambda b, side: project(b))

    scale = 1.0 / jnp.sqrt(jnp.float32(HD))

    def o_copy(j):
        dest = lax.rem(s + j, n)
        return remote(
            heads_out.at[dest], out.at[:, pl.ds(pl.multiple_of(s * HD, HD), HD)],
            o_send.at[j - 1], o_recv.at[j - 1], seq=dest,
        )

    def o_arrival(j):
        owner = lax.rem(s + n - j, n)
        here = out.at[:, pl.ds(pl.multiple_of(owner * HD, HD), HD)]
        return remote(heads_out.at[owner], here, o_send.at[j - 1], o_recv.at[j - 1], seq=owner)

    @pl.loop(1, n + 1)
    def _(j):
        b = lax.rem(s + j, n)
        query = qkv[pl.ds(pl.multiple_of(b * block, block), block), pl.ds(0, HD)]
        keys = qkv[:, pl.ds(HD, HD)]
        values = qkv[:, pl.ds(2 * HD, HD)]
        scores = lax.dot_general(
            query, keys, (((1,), (1,)), ((), ())), preferred_element_type=jnp.float32
        ) * scale
        expos = jnp.exp(scores - jnp.max(scores, axis=-1, keepdims=True))
        total = jnp.sum(expos, axis=-1, keepdims=True)
        summed = jnp.dot(expos.astype(jnp.bfloat16), values, preferred_element_type=jnp.float32)
        heads_out[b] = (summed / total).astype(jnp.bfloat16)
        pl.when(j < n)(lambda: o_copy(j).start())

    own_out = pltpu.make_async_copy(
        heads_out.at[s], out.at[:, pl.ds(pl.multiple_of(s * HD, HD), HD)], local_sem.at[0]
    )
    own_out.start()

    for j in range(1, n):
        for i in range(3):
            w_copy(j, i).wait_send()
        y_copy(j).wait_send()

    @pl.loop(0, n)
    def _(b):
        @pl.loop(0, CHUNKS)
        def _(k):
            pl.when((s < n - 1) & (b <= s))(lambda: up_copy(b, k).wait_send())
            pl.when((s > 0) & (b >= s))(lambda: down_copy(b, k).wait_send())
            x_copy(b, k).wait_send()
            c_copy(b, k, 0).wait_send()
            c_copy(b, k, 1).wait_send()

    own_out.wait()
    for j in range(1, n):
        o_copy(j).wait_send()
        o_arrival(j).wait_recv()


def one_head_per_device(acts, w_query, w_key, w_value):
    n = lax.axis_size("seq")
    rows, half_width = acts.shape
    depth, width = w_query.shape
    tokens = n * 2 * rows
    dma = pltpu.SemaphoreType.DMA
    anywhere = pl.BlockSpec(memory_space=pl.ANY)
    flops = 2 * tokens * depth * n * 3 * HD + 4 * tokens * tokens * HD
    return pl.pallas_call(
        functools.partial(head_kernel, n),
        out_shape=jax.ShapeDtypeStruct((2 * rows, width), jnp.bfloat16),
        in_specs=[anywhere] * 4,
        out_specs=anywhere,
        scratch_shapes=[
            pltpu.VMEM((n, 2, 2 * rows, half_width), jnp.bfloat16),
            pltpu.VMEM((n * depth, 3 * HD), jnp.bfloat16),
            pltpu.VMEM((tokens, 3 * HD), jnp.bfloat16),
            pltpu.VMEM((n, 2 * rows, HD), jnp.bfloat16),
            dma((4,)),
            dma((n - 1, 3)), dma((n - 1, 3)), dma((n - 1,)), dma((n - 1,)),
            dma((n, CHUNKS)), dma((n, CHUNKS)), dma((n, CHUNKS)),
            dma((n, CHUNKS)), dma((n, CHUNKS)),
            dma((2, n, CHUNKS)), dma((2, n, CHUNKS)),
            dma((n - 1,)), dma((n - 1,)),
        ],
        compiler_params=pltpu.CompilerParams(
            collective_id=0, has_side_effects=True, vmem_limit_bytes=48 * 1024 * 1024
        ),
        cost_estimate=pl.CostEstimate(flops=flops, bytes_accessed=2 * tokens * half_width, transcendentals=tokens * tokens),
    )(acts, w_query, w_key, w_value)


def passed_along(block, axis, distance):
    devices = range(lax.axis_size(axis))
    route = [((i - distance) % len(devices), i) for i in devices]
    return lax.ppermute(block, axis, route)


def blocks_passed_along(acts, w_query, w_key, w_value):
    block = lax.all_gather(acts, "row", axis=0, tiled=True)
    block = lax.all_gather(block, "col", axis=1, tiled=True)
    tokens_here = block.shape[0]
    width = w_query.shape[1]
    heads_here = width // HD
    pieces = (
        lax.all_gather(w_query, "seq", axis=0, tiled=True),
        lax.all_gather(w_key, "seq", axis=0, tiled=True),
        lax.all_gather(w_value, "seq", axis=0, tiled=True),
    )
    query_sum, key_sum, value_sum = tuple(
        (jnp.dot(block, piece, preferred_element_type=jnp.float32) for piece in pieces)
    )
    query = query_sum.astype(jnp.bfloat16).reshape(tokens_here, heads_here, HD)
    packed = jnp.stack([key_sum.astype(jnp.bfloat16), value_sum.astype(jnp.bfloat16)])
    blocks_seen = [packed]
    current = packed
    for step in range(1, SPAN):
        current = passed_along(current, "seq", 1)
        blocks_seen.append(current)
    scale = 1.0 / jnp.sqrt(jnp.float32(HD))
    score_list = []
    for seen in blocks_seen:
        seen_keys = seen[0].reshape(-1, heads_here, HD)
        score_list.append(
            jnp.einsum("qhd,khd->hqk", query, seen_keys, preferred_element_type=jnp.float32) * scale
        )
    largest = score_list[0].max(axis=-1, keepdims=True)
    for scores in score_list[1:]:
        largest = jnp.maximum(largest, scores.max(axis=-1, keepdims=True))
    running_total = jnp.zeros((heads_here, tokens_here), jnp.float32)
    summed = jnp.zeros((tokens_here, heads_here, HD), jnp.float32)
    for scores, seen in zip(score_list, blocks_seen):
        expos = jnp.exp(scores - largest)
        running_total = running_total + jnp.sum(expos, axis=-1)
        seen_values = seen[1].reshape(-1, heads_here, HD)
        summed = summed + jnp.einsum(
            "hqk,khd->qhd",
            expos.astype(jnp.bfloat16),
            seen_values,
            preferred_element_type=jnp.float32,
        )
    attended = summed / jnp.transpose(running_total)[:, :, None]
    return attended.astype(jnp.bfloat16).reshape(tokens_here, width)


def per_device(acts, w_query, w_key, w_value):
    n = lax.axis_size("seq")
    pairs = all(lax.axis_size(axis) == 2 for axis in ("groups", "row", "col"))
    depth, width = w_query.shape
    if pairs and n == SPAN and width == n * HD and acts.shape[0] % (16 * CHUNKS) == 0 and depth % 32 == 0:
        return one_head_per_device(acts, w_query, w_key, w_value)
    return blocks_passed_along(acts, w_query, w_key, w_value)


def solution(mesh):
    in_specs = (
        P(("groups", "seq", "row"), "col"),
        P("seq", ("row", "col")),
        P("seq", ("row", "col")),
        P("seq", ("row", "col")),
    )
    out_specs = P(("groups", "seq"), ("row", "col"))
    return jax.shard_map(
        per_device, mesh=mesh, in_specs=in_specs, out_specs=out_specs, check_vma=False
    )
```

```python
import functools

import jax
import jax.numpy as jnp
from jax import lax
from jax.experimental import pallas as pl
from jax.experimental.pallas import tpu as pltpu
from jax.sharding import PartitionSpec as P

HD = 128
SPAN = 4
CHUNKS = 4
MESH = pl.DeviceIdType.MESH


def head_kernel(
    n, acts, w_query, w_key, w_value, out,
    x_all, w_all, qkv, heads_out,
    local_sem, w_send, w_recv, y_send, y_recv,
    up_send, down_send, z_recv, x_send, x_recv, c_send, c_recv, o_send, o_recv,
):
    g, s = lax.axis_index("groups"), lax.axis_index("seq")
    r, c = lax.axis_index("row"), lax.axis_index("col")
    weights = (w_query, w_key, w_value)
    rows, half_width = acts.shape
    depth = w_query.shape[0]
    half = depth // 2
    block = 2 * rows
    part = rows // CHUNKS

    barrier = pltpu.get_barrier_semaphore()
    for j in range(1, n):
        pl.semaphore_signal(barrier, inc=1, device_id={"seq": lax.rem(s + j, n)}, device_id_type=MESH)
    pl.semaphore_signal(barrier, inc=1, device_id={"groups": 1 - g}, device_id_type=MESH)
    pl.semaphore_signal(barrier, inc=1, device_id={"row": 1 - r}, device_id_type=MESH)
    pl.semaphore_signal(barrier, inc=1, device_id={"col": 1 - c}, device_id_type=MESH)
    pl.semaphore_wait(barrier, n + 2)

    def remote(src, dst, send, recv, **device):
        return pltpu.make_async_remote_copy(
            src_ref=src, dst_ref=dst, send_sem=send, recv_sem=recv, device_id=device, device_id_type=MESH
        )

    def w_rows(owner, which):
        return pl.ds(pl.multiple_of(owner * depth + which * half, half), half)

    def w_copy(j, i):
        dest = lax.rem(s + j, n)
        return remote(
            weights[i].at[pl.ds(pl.multiple_of(g * half, half), half), pl.ds(pl.multiple_of(dest * HD, HD), HD)],
            w_all.at[w_rows(s, g), pl.ds(i * HD, HD)],
            w_send.at[j - 1, i], w_recv.at[j - 1, i], seq=dest,
        )

    def w_arrival(j, i):
        owner = lax.rem(s + n - j, n)
        here = w_all.at[w_rows(owner, g), pl.ds(i * HD, HD)]
        return remote(here, here, w_send.at[j - 1, i], w_recv.at[j - 1, i], seq=lax.rem(s + j, n))

    def y_copy(j, i, which=g):
        owner = lax.rem(s + n - j, n)
        here = w_all.at[w_rows(owner, which), pl.ds(i * HD, HD)]
        return remote(here, here, y_send.at[j - 1, i], y_recv.at[j - 1, i], groups=1 - g)

    def y_arrival(j, i):
        return y_copy(j, i, 1 - g)

    def spot(b, rr, cc, k):
        return x_all.at[b, cc, pl.ds(pl.multiple_of(rr * rows + k * part, part), part), :]

    def source(b, k, own):
        return acts.at[pl.ds(pl.multiple_of(k * part, part), part), :] if own else spot(b, r, c, k)

    def up_copy(b, k, own=False):
        return remote(source(b, k, own), spot(b, r, c, k), up_send.at[b, k], z_recv.at[b, k], seq=s + 1)

    def down_copy(b, k, own=False):
        return remote(source(b, k, own), spot(b, r, c, k), down_send.at[b, k], z_recv.at[b, k], seq=s - 1)

    def x_copy(b, k, own=False):
        return remote(source(b, k, own), spot(b, r, c, k), x_send.at[b, k], x_recv.at[b, k], row=1 - r)

    def x_arrival(b, k):
        here = spot(b, 1 - r, c, k)
        return remote(here, here, x_send.at[b, k], x_recv.at[b, k], row=1 - r)

    def c_copy(b, k, rr, own=False):
        src = source(b, k, True) if own else spot(b, rr, c, k)
        return remote(src, spot(b, rr, c, k), c_send.at[rr, b, k], c_recv.at[rr, b, k], col=1 - c)

    def c_arrival(b, k, rr):
        here = spot(b, rr, 1 - c, k)
        return remote(here, here, c_send.at[rr, b, k], c_recv.at[rr, b, k], col=1 - c)

    for i in range(3):
        for j in range(1, n):
            w_copy(j, i).start()

    @pl.loop(0, CHUNKS)
    def _(k):
        @pl.when(s < n - 1)
        def _():
            up_copy(s, k, True).start()

        @pl.when(s > 0)
        def _():
            down_copy(s, k, True).start()

        x_copy(s, k, True).start()
        c_copy(s, k, r, True).start()

    own_copies = [
        pltpu.make_async_copy(
            acts, x_all.at[s, c, pl.ds(pl.multiple_of(r * rows, rows), rows), :], local_sem.at[0]
        )
    ] + [
        pltpu.make_async_copy(
            weights[i].at[:, pl.ds(pl.multiple_of(s * HD, HD), HD)],
            w_all.at[pl.ds(pl.multiple_of(s * depth, depth), depth), pl.ds(i * HD, HD)],
            local_sem.at[1 + i],
        )
        for i in range(3)
    ]
    for copy in own_copies:
        copy.start()

    def each_at(t, body):
        if t == 0:
            body(s, 0)
            return
        pl.when(s - t >= 0)(lambda: body(s - t, 1))
        pl.when(s + t < n)(lambda: body(s + t, -1))

    def pass_on(b, side, k):
        here = spot(b, r, c, k)
        remote(here, here, up_send.at[b, k], z_recv.at[b, k], row=1 - r).wait_recv()
        if side > 0:
            pl.when(s < n - 1)(lambda: up_copy(b, k).start())
        else:
            pl.when(s > 0)(lambda: down_copy(b, k).start())
        x_copy(b, k).start()
        c_copy(b, k, r).start()

    def across(b, k):
        x_arrival(b, k).wait_recv()
        c_copy(b, k, 1 - r).start()

    def project(t):
        @pl.loop(0, 2 if t else 1)
        def _(side):
            b = s + (2 * side - 1) * t

            @pl.when((b >= 0) & (b < n))
            def _():
                @pl.loop(0, CHUNKS)
                def _(k):
                    c_arrival(b, k, 0).wait_recv()
                    c_arrival(b, k, 1).wait_recv()

                total = jnp.dot(x_all[b, 0], w_all[:half_width, :], preferred_element_type=jnp.float32)
                total += jnp.dot(x_all[b, 1], w_all[half_width:, :], preferred_element_type=jnp.float32)
                qkv[pl.ds(pl.multiple_of(b * block, block), block), :] = total.astype(jnp.bfloat16)

    for t in range(1, n):
        for k in range(CHUNKS):
            each_at(t, lambda b, side: pass_on(b, side, k))
            each_at(t - 1, lambda b, side: across(b, k))
            if t == 1 and 1 <= k <= 3:
                for j in range(1, n):
                    w_arrival(j, k - 1).wait_recv()
                    y_copy(j, k - 1).start()
            if t == n - 1 and k == 0:
                for copy in own_copies:
                    copy.wait()
                for j in range(1, n):
                    for i in range(3):
                        y_arrival(j, i).wait_recv()
            if t == n - 1 and k < n - 2:
                project(k)
    project(n - 2)

    @pl.loop(0, CHUNKS)
    def _(k):
        each_at(n - 1, lambda b, side: across(b, k))

    project(n - 1)

    scale = 1.0 / jnp.sqrt(jnp.float32(HD))

    def o_copy(j):
        dest = lax.rem(s + j, n)
        return remote(
            heads_out.at[dest], out.at[:, pl.ds(pl.multiple_of(s * HD, HD), HD)],
            o_send.at[j - 1], o_recv.at[j - 1], seq=dest,
        )

    def o_arrival(j):
        owner = lax.rem(s + n - j, n)
        here = out.at[:, pl.ds(pl.multiple_of(owner * HD, HD), HD)]
        return remote(heads_out.at[owner], here, o_send.at[j - 1], o_recv.at[j - 1], seq=owner)

    @pl.loop(1, n + 1)
    def _(j):
        b = lax.rem(s + j, n)
        query = qkv[pl.ds(pl.multiple_of(b * block, block), block), pl.ds(0, HD)]
        keys = qkv[:, pl.ds(HD, HD)]
        values = qkv[:, pl.ds(2 * HD, HD)]
        scores = lax.dot_general(
            query, keys, (((1,), (1,)), ((), ())), preferred_element_type=jnp.float32
        ) * scale
        expos = jnp.exp(scores - jnp.max(scores, axis=-1, keepdims=True))
        total = jnp.sum(expos, axis=-1, keepdims=True)
        summed = jnp.dot(expos.astype(jnp.bfloat16), values, preferred_element_type=jnp.float32)
        heads_out[b] = (summed / total).astype(jnp.bfloat16)
        pl.when(j < n)(lambda: o_copy(j).start())

    own_out = pltpu.make_async_copy(
        heads_out.at[s], out.at[:, pl.ds(pl.multiple_of(s * HD, HD), HD)], local_sem.at[0]
    )
    own_out.start()

    for j in range(1, n):
        for i in range(3):
            w_copy(j, i).wait_send()
            y_copy(j, i).wait_send()

    @pl.loop(0, n)
    def _(b):
        @pl.loop(0, CHUNKS)
        def _(k):
            pl.when((s < n - 1) & (b <= s))(lambda: up_copy(b, k).wait_send())
            pl.when((s > 0) & (b >= s))(lambda: down_copy(b, k).wait_send())
            x_copy(b, k).wait_send()
            c_copy(b, k, 0).wait_send()
            c_copy(b, k, 1).wait_send()

    own_out.wait()
    for j in range(1, n):
        o_copy(j).wait_send()
        o_arrival(j).wait_recv()


def one_head_per_device(acts, w_query, w_key, w_value):
    n = lax.axis_size("seq")
    rows, half_width = acts.shape
    depth, width = w_query.shape
    tokens = n * 2 * rows
    dma = pltpu.SemaphoreType.DMA
    flops = 2 * tokens * depth * n * 3 * HD + 4 * tokens * tokens * HD
    return pl.pallas_call(
        functools.partial(head_kernel, n),
        out_shape=jax.ShapeDtypeStruct((2 * rows, width), jnp.bfloat16),
        in_specs=[pl.BlockSpec(memory_space=pl.ANY)] * 4,
        out_specs=pl.BlockSpec(memory_space=pl.ANY),
        scratch_shapes=[
            pltpu.VMEM((n, 2, 2 * rows, half_width), jnp.bfloat16),
            pltpu.VMEM((n * depth, 3 * HD), jnp.bfloat16),
            pltpu.VMEM((tokens, 3 * HD), jnp.bfloat16),
            pltpu.VMEM((n, 2 * rows, HD), jnp.bfloat16),
            dma((4,)),
            dma((n - 1, 3)), dma((n - 1, 3)), dma((n - 1, 3)), dma((n - 1, 3)),
            dma((n, CHUNKS)), dma((n, CHUNKS)), dma((n, CHUNKS)),
            dma((n, CHUNKS)), dma((n, CHUNKS)),
            dma((2, n, CHUNKS)), dma((2, n, CHUNKS)),
            dma((n - 1,)), dma((n - 1,)),
        ],
        compiler_params=pltpu.CompilerParams(
            collective_id=0, has_side_effects=True, vmem_limit_bytes=63 * 1024 * 1024
        ),
        cost_estimate=pl.CostEstimate(flops=flops, bytes_accessed=2 * tokens * half_width, transcendentals=tokens * tokens),
    )(acts, w_query, w_key, w_value)


def passed_along(block, axis, distance):
    devices = range(lax.axis_size(axis))
    route = [((i - distance) % len(devices), i) for i in devices]
    return lax.ppermute(block, axis, route)


def blocks_passed_along(acts, w_query, w_key, w_value):
    block = lax.all_gather(acts, "row", axis=0, tiled=True)
    block = lax.all_gather(block, "col", axis=1, tiled=True)
    tokens_here = block.shape[0]
    width = w_query.shape[1]
    heads_here = width // HD
    pieces = (
        lax.all_gather(w_query, "seq", axis=0, tiled=True),
        lax.all_gather(w_key, "seq", axis=0, tiled=True),
        lax.all_gather(w_value, "seq", axis=0, tiled=True),
    )
    query_sum, key_sum, value_sum = tuple(
        (jnp.dot(block, piece, preferred_element_type=jnp.float32) for piece in pieces)
    )
    query = query_sum.astype(jnp.bfloat16).reshape(tokens_here, heads_here, HD)
    packed = jnp.stack([key_sum.astype(jnp.bfloat16), value_sum.astype(jnp.bfloat16)])
    blocks_seen = [packed]
    current = packed
    for step in range(1, SPAN):
        current = passed_along(current, "seq", 1)
        blocks_seen.append(current)
    scale = 1.0 / jnp.sqrt(jnp.float32(HD))
    score_list = []
    for seen in blocks_seen:
        seen_keys = seen[0].reshape(-1, heads_here, HD)
        score_list.append(
            jnp.einsum("qhd,khd->hqk", query, seen_keys, preferred_element_type=jnp.float32) * scale
        )
    largest = score_list[0].max(axis=-1, keepdims=True)
    for scores in score_list[1:]:
        largest = jnp.maximum(largest, scores.max(axis=-1, keepdims=True))
    running_total = jnp.zeros((heads_here, tokens_here), jnp.float32)
    summed = jnp.zeros((tokens_here, heads_here, HD), jnp.float32)
    for scores, seen in zip(score_list, blocks_seen):
        expos = jnp.exp(scores - largest)
        running_total = running_total + jnp.sum(expos, axis=-1)
        seen_values = seen[1].reshape(-1, heads_here, HD)
        summed = summed + jnp.einsum(
            "hqk,khd->qhd",
            expos.astype(jnp.bfloat16),
            seen_values,
            preferred_element_type=jnp.float32,
        )
    attended = summed / jnp.transpose(running_total)[:, :, None]
    return attended.astype(jnp.bfloat16).reshape(tokens_here, width)


def per_device(acts, w_query, w_key, w_value):
    n = lax.axis_size("seq")
    pairs = all(lax.axis_size(axis) == 2 for axis in ("groups", "row", "col"))
    depth, width = w_query.shape
    if pairs and n == SPAN and width == n * HD and acts.shape[0] % (16 * CHUNKS) == 0 and depth % 32 == 0:
        return one_head_per_device(acts, w_query, w_key, w_value)
    return blocks_passed_along(acts, w_query, w_key, w_value)


def solution(mesh):
    in_specs = (
        P(("groups", "seq", "row"), "col"),
        P("seq", ("row", "col")),
        P("seq", ("row", "col")),
        P("seq", ("row", "col")),
    )
    out_specs = P(("groups", "seq"), ("row", "col"))
    return jax.shard_map(
        per_device, mesh=mesh, in_specs=in_specs, out_specs=out_specs, check_vma=False
    )
```

```python
import functools
import math

import jax
import jax.numpy as jnp
from jax import lax
from jax.experimental import pallas as pl
from jax.experimental.pallas import tpu as pltpu
from jax.sharding import PartitionSpec as P

HD = 128
SPAN = 4
CHUNKS = 6
MESH = pl.DeviceIdType.MESH


def head_kernel(
    n, acts, w_query, w_key, w_value, out,
    x_all, w_all, qkv, heads_out,
    local_sem, w_send, w_recv, y_send, y_recv,
    up_send, down_send, z_recv, x_send, x_recv, c_send, c_recv, o_send, o_recv,
):
    g, s = lax.axis_index("groups"), lax.axis_index("seq")
    r, c = lax.axis_index("row"), lax.axis_index("col")
    weights = (w_query, w_key, w_value)
    rows, half_width = acts.shape
    depth = w_query.shape[0]
    half = depth // 2
    block = 2 * rows
    part = rows // CHUNKS

    barrier = pltpu.get_barrier_semaphore()
    for j in range(1, n):
        pl.semaphore_signal(barrier, inc=1, device_id={"seq": lax.rem(s + j, n)}, device_id_type=MESH)
    pl.semaphore_signal(barrier, inc=1, device_id={"groups": 1 - g}, device_id_type=MESH)
    pl.semaphore_signal(barrier, inc=1, device_id={"row": 1 - r}, device_id_type=MESH)
    pl.semaphore_signal(barrier, inc=1, device_id={"col": 1 - c}, device_id_type=MESH)
    pl.semaphore_wait(barrier, n + 2)

    def remote(src, dst, send, recv, **device):
        return pltpu.make_async_remote_copy(
            src_ref=src, dst_ref=dst, send_sem=send, recv_sem=recv, device_id=device, device_id_type=MESH
        )

    def w_rows(owner, which):
        return pl.ds(pl.multiple_of(owner * depth + which * half, half), half)

    def w_copy(j, i):
        dest = lax.rem(s + j, n)
        return remote(
            weights[i].at[pl.ds(pl.multiple_of(g * half, half), half), pl.ds(pl.multiple_of(dest * HD, HD), HD)],
            w_all.at[w_rows(s, g), pl.ds(i * HD, HD)],
            w_send.at[j - 1, i], w_recv.at[j - 1, i], seq=dest,
        )

    def w_arrival(j, i):
        owner = lax.rem(s + n - j, n)
        here = w_all.at[w_rows(owner, g), pl.ds(i * HD, HD)]
        return remote(here, here, w_send.at[j - 1, i], w_recv.at[j - 1, i], seq=lax.rem(s + j, n))

    def y_copy(j, i, which=g):
        owner = lax.rem(s + n - j, n)
        here = w_all.at[w_rows(owner, which), pl.ds(i * HD, HD)]
        return remote(here, here, y_send.at[j - 1, i], y_recv.at[j - 1, i], groups=1 - g)

    def y_arrival(j, i):
        return y_copy(j, i, 1 - g)

    def spot(b, rr, cc, k):
        return x_all.at[b, cc, pl.ds(pl.multiple_of(rr * rows + k * part, part), part), :]

    def source(b, k, own):
        return acts.at[pl.ds(pl.multiple_of(k * part, part), part), :] if own else spot(b, r, c, k)

    def up_copy(b, k, own=False):
        return remote(source(b, k, own), spot(b, r, c, k), up_send.at[b, k], z_recv.at[b, k], seq=s + 1)

    def down_copy(b, k, own=False):
        return remote(source(b, k, own), spot(b, r, c, k), down_send.at[b, k], z_recv.at[b, k], seq=s - 1)

    def x_copy(b, k, own=False):
        return remote(source(b, k, own), spot(b, r, c, k), x_send.at[b, k], x_recv.at[b, k], row=1 - r)

    def x_arrival(b, k):
        here = spot(b, 1 - r, c, k)
        return remote(here, here, x_send.at[b, k], x_recv.at[b, k], row=1 - r)

    def c_copy(b, k, rr, own=False):
        src = source(b, k, True) if own else spot(b, rr, c, k)
        return remote(src, spot(b, rr, c, k), c_send.at[rr, b, k], c_recv.at[rr, b, k], col=1 - c)

    def c_arrival(b, k, rr):
        here = spot(b, rr, 1 - c, k)
        return remote(here, here, c_send.at[rr, b, k], c_recv.at[rr, b, k], col=1 - c)

    for i in range(3):
        for j in range(1, n):
            w_copy(j, i).start()

    @pl.loop(0, CHUNKS)
    def _(k):
        @pl.when(s < n - 1)
        def _():
            up_copy(s, k, True).start()

        @pl.when(s > 0)
        def _():
            down_copy(s, k, True).start()

        x_copy(s, k, True).start()
        c_copy(s, k, r, True).start()

    own_copies = [
        pltpu.make_async_copy(
            acts, x_all.at[s, c, pl.ds(pl.multiple_of(r * rows, rows), rows), :], local_sem.at[0]
        )
    ] + [
        pltpu.make_async_copy(
            weights[i].at[:, pl.ds(pl.multiple_of(s * HD, HD), HD)],
            w_all.at[pl.ds(pl.multiple_of(s * depth, depth), depth), pl.ds(i * HD, HD)],
            local_sem.at[1 + i],
        )
        for i in range(3)
    ]
    for copy in own_copies:
        copy.start()

    def each_at(t, body):
        if t == 0:
            body(s, 0)
            return
        pl.when(s - t >= 0)(lambda: body(s - t, 1))
        pl.when(s + t < n)(lambda: body(s + t, -1))

    def pass_on(b, side, k):
        here = spot(b, r, c, k)
        remote(here, here, up_send.at[b, k], z_recv.at[b, k], row=1 - r).wait_recv()
        if side > 0:
            pl.when(s < n - 1)(lambda: up_copy(b, k).start())
        else:
            pl.when(s > 0)(lambda: down_copy(b, k).start())
        x_copy(b, k).start()
        c_copy(b, k, r).start()

    def across(b, k):
        x_arrival(b, k).wait_recv()
        c_copy(b, k, 1 - r).start()

    def project(t):
        @pl.loop(0, 2 if t else 1)
        def _(side):
            b = s + (2 * side - 1) * t

            @pl.when((b >= 0) & (b < n))
            def _():
                @pl.loop(0, CHUNKS)
                def _(k):
                    c_arrival(b, k, 0).wait_recv()
                    c_arrival(b, k, 1).wait_recv()

                total = jnp.dot(x_all[b, 0], w_all[:half_width, :], preferred_element_type=jnp.float32)
                total += jnp.dot(x_all[b, 1], w_all[half_width:, :], preferred_element_type=jnp.float32)
                qkv[pl.ds(pl.multiple_of(b * block, block), block), :] = total.astype(jnp.bfloat16)

    for t in range(1, n):
        for k in range(CHUNKS):
            each_at(t, lambda b, side: pass_on(b, side, k))
            each_at(t - 1, lambda b, side: across(b, k))
            if t == 1 and 1 <= k <= 3:
                for j in range(1, n):
                    w_arrival(j, k - 1).wait_recv()
                    y_copy(j, k - 1).start()
            if t == n - 1 and k == 0:
                for copy in own_copies:
                    copy.wait()
                for j in range(1, n):
                    for i in range(3):
                        y_arrival(j, i).wait_recv()
            if t == n - 1 and k < n - 2:
                project(k)
    project(n - 2)

    @pl.loop(0, CHUNKS)
    def _(k):
        each_at(n - 1, lambda b, side: across(b, k))

    project(n - 1)

    rate = math.log2(math.e) / math.sqrt(HD)

    def o_copy(j):
        dest = lax.rem(s + j, n)
        return remote(
            heads_out.at[dest], out.at[:, pl.ds(pl.multiple_of(s * HD, HD), HD)],
            o_send.at[j - 1], o_recv.at[j - 1], seq=dest,
        )

    def o_arrival(j):
        owner = lax.rem(s + n - j, n)
        here = out.at[:, pl.ds(pl.multiple_of(owner * HD, HD), HD)]
        return remote(heads_out.at[owner], here, o_send.at[j - 1], o_recv.at[j - 1], seq=owner)

    @pl.loop(1, n + 1)
    def _(j):
        b = lax.rem(s + j, n)
        query = qkv[pl.ds(pl.multiple_of(b * block, block), block), pl.ds(0, HD)]
        keys = qkv[:, pl.ds(HD, HD)]
        values = qkv[:, pl.ds(2 * HD, HD)]
        scores = lax.dot_general(
            query, keys, (((1,), (1,)), ((), ())), preferred_element_type=jnp.float32
        )
        expos = jnp.exp2((scores - jnp.max(scores, axis=-1, keepdims=True)) * rate)
        total = jnp.sum(expos, axis=-1, keepdims=True)
        summed = jnp.dot(expos.astype(jnp.bfloat16), values, preferred_element_type=jnp.float32)
        heads_out[b] = (summed / total).astype(jnp.bfloat16)
        pl.when(j < n)(lambda: o_copy(j).start())

    own_out = pltpu.make_async_copy(
        heads_out.at[s], out.at[:, pl.ds(pl.multiple_of(s * HD, HD), HD)], local_sem.at[0]
    )
    own_out.start()

    for j in range(1, n):
        for i in range(3):
            w_copy(j, i).wait_send()
            y_copy(j, i).wait_send()

    @pl.loop(0, n)
    def _(b):
        @pl.loop(0, CHUNKS)
        def _(k):
            pl.when((s < n - 1) & (b <= s))(lambda: up_copy(b, k).wait_send())
            pl.when((s > 0) & (b >= s))(lambda: down_copy(b, k).wait_send())
            x_copy(b, k).wait_send()
            c_copy(b, k, 0).wait_send()
            c_copy(b, k, 1).wait_send()

    own_out.wait()
    for j in range(1, n):
        o_copy(j).wait_send()
        o_arrival(j).wait_recv()


def one_head_per_device(acts, w_query, w_key, w_value):
    n = lax.axis_size("seq")
    rows, half_width = acts.shape
    depth, width = w_query.shape
    tokens = n * 2 * rows
    dma = pltpu.SemaphoreType.DMA
    flops = 2 * tokens * depth * n * 3 * HD + 4 * tokens * tokens * HD
    return pl.pallas_call(
        functools.partial(head_kernel, n),
        out_shape=jax.ShapeDtypeStruct((2 * rows, width), jnp.bfloat16),
        in_specs=[pl.BlockSpec(memory_space=pl.ANY)] * 4,
        out_specs=pl.BlockSpec(memory_space=pl.ANY),
        scratch_shapes=[
            pltpu.VMEM((n, 2, 2 * rows, half_width), jnp.bfloat16),
            pltpu.VMEM((n * depth, 3 * HD), jnp.bfloat16),
            pltpu.VMEM((tokens, 3 * HD), jnp.bfloat16),
            pltpu.VMEM((n, 2 * rows, HD), jnp.bfloat16),
            dma((4,)),
            dma((n - 1, 3)), dma((n - 1, 3)), dma((n - 1, 3)), dma((n - 1, 3)),
            dma((n, CHUNKS)), dma((n, CHUNKS)), dma((n, CHUNKS)),
            dma((n, CHUNKS)), dma((n, CHUNKS)),
            dma((2, n, CHUNKS)), dma((2, n, CHUNKS)),
            dma((n - 1,)), dma((n - 1,)),
        ],
        compiler_params=pltpu.CompilerParams(
            collective_id=0, has_side_effects=True, vmem_limit_bytes=63 * 1024 * 1024
        ),
        cost_estimate=pl.CostEstimate(flops=flops, bytes_accessed=2 * tokens * half_width, transcendentals=tokens * tokens),
    )(acts, w_query, w_key, w_value)


def passed_along(block, axis, distance):
    devices = range(lax.axis_size(axis))
    route = [((i - distance) % len(devices), i) for i in devices]
    return lax.ppermute(block, axis, route)


def blocks_passed_along(acts, w_query, w_key, w_value):
    block = lax.all_gather(acts, "row", axis=0, tiled=True)
    block = lax.all_gather(block, "col", axis=1, tiled=True)
    tokens_here = block.shape[0]
    width = w_query.shape[1]
    heads_here = width // HD
    pieces = (
        lax.all_gather(w_query, "seq", axis=0, tiled=True),
        lax.all_gather(w_key, "seq", axis=0, tiled=True),
        lax.all_gather(w_value, "seq", axis=0, tiled=True),
    )
    query_sum, key_sum, value_sum = tuple(
        (jnp.dot(block, piece, preferred_element_type=jnp.float32) for piece in pieces)
    )
    query = query_sum.astype(jnp.bfloat16).reshape(tokens_here, heads_here, HD)
    packed = jnp.stack([key_sum.astype(jnp.bfloat16), value_sum.astype(jnp.bfloat16)])
    blocks_seen = [packed]
    current = packed
    for step in range(1, SPAN):
        current = passed_along(current, "seq", 1)
        blocks_seen.append(current)
    scale = 1.0 / jnp.sqrt(jnp.float32(HD))
    score_list = []
    for seen in blocks_seen:
        seen_keys = seen[0].reshape(-1, heads_here, HD)
        score_list.append(
            jnp.einsum("qhd,khd->hqk", query, seen_keys, preferred_element_type=jnp.float32) * scale
        )
    largest = score_list[0].max(axis=-1, keepdims=True)
    for scores in score_list[1:]:
        largest = jnp.maximum(largest, scores.max(axis=-1, keepdims=True))
    running_total = jnp.zeros((heads_here, tokens_here), jnp.float32)
    summed = jnp.zeros((tokens_here, heads_here, HD), jnp.float32)
    for scores, seen in zip(score_list, blocks_seen):
        expos = jnp.exp(scores - largest)
        running_total = running_total + jnp.sum(expos, axis=-1)
        seen_values = seen[1].reshape(-1, heads_here, HD)
        summed = summed + jnp.einsum(
            "hqk,khd->qhd",
            expos.astype(jnp.bfloat16),
            seen_values,
            preferred_element_type=jnp.float32,
        )
    attended = summed / jnp.transpose(running_total)[:, :, None]
    return attended.astype(jnp.bfloat16).reshape(tokens_here, width)


def per_device(acts, w_query, w_key, w_value):
    n = lax.axis_size("seq")
    pairs = all(lax.axis_size(axis) == 2 for axis in ("groups", "row", "col"))
    depth, width = w_query.shape
    if pairs and n == SPAN and width == n * HD and acts.shape[0] % (16 * CHUNKS) == 0 and depth % 32 == 0:
        return one_head_per_device(acts, w_query, w_key, w_value)
    return blocks_passed_along(acts, w_query, w_key, w_value)


def solution(mesh):
    in_specs = (
        P(("groups", "seq", "row"), "col"),
        P("seq", ("row", "col")),
        P("seq", ("row", "col")),
        P("seq", ("row", "col")),
    )
    out_specs = P(("groups", "seq"), ("row", "col"))
    return jax.shard_map(
        per_device, mesh=mesh, in_specs=in_specs, out_specs=out_specs, check_vma=False
    )
```

```python
import functools
import math

import jax
import jax.numpy as jnp
from jax import lax
from jax.experimental import pallas as pl
from jax.experimental.pallas import tpu as pltpu
from jax.sharding import PartitionSpec as P

HD = 128
SPAN = 4
CHUNKS = 6
MESH = pl.DeviceIdType.MESH


def head_kernel(
    n, acts, w_query, w_key, w_value, out,
    x_all, w_all, qkv, heads_out, tops, totals, sums,
    local_sem, w_send, w_recv, y_send, y_recv,
    up_send, down_send, z_recv, x_send, x_recv, c_send, c_recv, o_send, o_recv,
):
    g, s = lax.axis_index("groups"), lax.axis_index("seq")
    r, c = lax.axis_index("row"), lax.axis_index("col")
    weights = (w_query, w_key, w_value)
    rows, half_width = acts.shape
    depth = w_query.shape[0]
    half = depth // 2
    block = 2 * rows
    part = rows // CHUNKS

    barrier = pltpu.get_barrier_semaphore()
    for j in range(1, n):
        pl.semaphore_signal(barrier, inc=1, device_id={"seq": lax.rem(s + j, n)}, device_id_type=MESH)
    pl.semaphore_signal(barrier, inc=1, device_id={"groups": 1 - g}, device_id_type=MESH)
    pl.semaphore_signal(barrier, inc=1, device_id={"row": 1 - r}, device_id_type=MESH)
    pl.semaphore_signal(barrier, inc=1, device_id={"col": 1 - c}, device_id_type=MESH)
    pl.semaphore_wait(barrier, n + 2)

    def remote(src, dst, send, recv, **device):
        return pltpu.make_async_remote_copy(
            src_ref=src, dst_ref=dst, send_sem=send, recv_sem=recv, device_id=device, device_id_type=MESH
        )

    def w_rows(owner, which):
        return pl.ds(pl.multiple_of(owner * depth + which * half, half), half)

    def w_copy(j, i):
        dest = lax.rem(s + j, n)
        return remote(
            weights[i].at[pl.ds(pl.multiple_of(g * half, half), half), pl.ds(pl.multiple_of(dest * HD, HD), HD)],
            w_all.at[w_rows(s, g), pl.ds(i * HD, HD)],
            w_send.at[j - 1, i], w_recv.at[j - 1, i], seq=dest,
        )

    def w_arrival(j, i):
        owner = lax.rem(s + n - j, n)
        here = w_all.at[w_rows(owner, g), pl.ds(i * HD, HD)]
        return remote(here, here, w_send.at[j - 1, i], w_recv.at[j - 1, i], seq=lax.rem(s + j, n))

    def y_copy(j, i, which=g):
        owner = lax.rem(s + n - j, n)
        here = w_all.at[w_rows(owner, which), pl.ds(i * HD, HD)]
        return remote(here, here, y_send.at[j - 1, i], y_recv.at[j - 1, i], groups=1 - g)

    def y_arrival(j, i):
        return y_copy(j, i, 1 - g)

    def spot(b, rr, cc, k):
        return x_all.at[b, cc, pl.ds(pl.multiple_of(rr * rows + k * part, part), part), :]

    def source(b, k, own):
        return acts.at[pl.ds(pl.multiple_of(k * part, part), part), :] if own else spot(b, r, c, k)

    def up_copy(b, k, own=False):
        return remote(source(b, k, own), spot(b, r, c, k), up_send.at[b, k], z_recv.at[b, k], seq=s + 1)

    def down_copy(b, k, own=False):
        return remote(source(b, k, own), spot(b, r, c, k), down_send.at[b, k], z_recv.at[b, k], seq=s - 1)

    def x_copy(b, k, own=False):
        return remote(source(b, k, own), spot(b, r, c, k), x_send.at[b, k], x_recv.at[b, k], row=1 - r)

    def x_arrival(b, k):
        here = spot(b, 1 - r, c, k)
        return remote(here, here, x_send.at[b, k], x_recv.at[b, k], row=1 - r)

    def c_copy(b, k, rr, own=False):
        src = source(b, k, True) if own else spot(b, rr, c, k)
        return remote(src, spot(b, rr, c, k), c_send.at[rr, b, k], c_recv.at[rr, b, k], col=1 - c)

    def c_arrival(b, k, rr):
        here = spot(b, rr, 1 - c, k)
        return remote(here, here, c_send.at[rr, b, k], c_recv.at[rr, b, k], col=1 - c)

    for i in range(3):
        for j in range(1, n):
            w_copy(j, i).start()

    @pl.loop(0, CHUNKS)
    def _(k):
        @pl.when(s < n - 1)
        def _():
            up_copy(s, k, True).start()

        @pl.when(s > 0)
        def _():
            down_copy(s, k, True).start()

        x_copy(s, k, True).start()
        c_copy(s, k, r, True).start()

    own_copies = [
        pltpu.make_async_copy(
            acts, x_all.at[s, c, pl.ds(pl.multiple_of(r * rows, rows), rows), :], local_sem.at[0]
        )
    ] + [
        pltpu.make_async_copy(
            weights[i].at[:, pl.ds(pl.multiple_of(s * HD, HD), HD)],
            w_all.at[pl.ds(pl.multiple_of(s * depth, depth), depth), pl.ds(i * HD, HD)],
            local_sem.at[1 + i],
        )
        for i in range(3)
    ]
    for copy in own_copies:
        copy.start()

    def each_at(t, body):
        if t == 0:
            body(s, 0)
            return
        pl.when(s - t >= 0)(lambda: body(s - t, 1))
        pl.when(s + t < n)(lambda: body(s + t, -1))

    def pass_on(b, side, k):
        here = spot(b, r, c, k)
        remote(here, here, up_send.at[b, k], z_recv.at[b, k], row=1 - r).wait_recv()
        if side > 0:
            pl.when(s < n - 1)(lambda: up_copy(b, k).start())
        else:
            pl.when(s > 0)(lambda: down_copy(b, k).start())
        x_copy(b, k).start()
        c_copy(b, k, r).start()

    def across(b, k):
        x_arrival(b, k).wait_recv()
        c_copy(b, k, 1 - r).start()

    def project(t):
        @pl.loop(0, 2 if t else 1)
        def _(side):
            b = s + (2 * side - 1) * t

            @pl.when((b >= 0) & (b < n))
            def _():
                @pl.loop(0, CHUNKS)
                def _(k):
                    c_arrival(b, k, 0).wait_recv()
                    c_arrival(b, k, 1).wait_recv()

                total = jnp.dot(x_all[b, 0], w_all[:half_width, :], preferred_element_type=jnp.float32)
                total += jnp.dot(x_all[b, 1], w_all[half_width:, :], preferred_element_type=jnp.float32)
                qkv[pl.ds(pl.multiple_of(b * block, block), block), :] = total.astype(jnp.bfloat16)

    rate = math.log2(math.e) / math.sqrt(HD)
    at_end = (s == 0) | (s == n - 1)
    far = n - 1 - s

    def of_block(b, what):
        return qkv[pl.ds(pl.multiple_of(b * block, block), block), pl.ds(what * HD, HD)]

    def scores_of(query, keys):
        return lax.dot_general(query, keys, (((1,), (1,)), ((), ())), preferred_element_type=jnp.float32)

    def weigh(scores, top, values):
        expos = jnp.exp2((scores - top) * rate)
        summed = jnp.dot(expos.astype(jnp.bfloat16), values, preferred_element_type=jnp.float32)
        return jnp.sum(expos, axis=-1, keepdims=True), summed

    def attend_near(i):
        @pl.when(at_end)
        def _():
            b = jnp.where(s == 0, i, n - 1 - i)
            near = pl.ds(pl.multiple_of(jnp.where(s == 0, 0, block), block), (n - 1) * block)
            scores = scores_of(of_block(b, 0), qkv[near, pl.ds(HD, HD)])
            top = jnp.max(scores, axis=-1, keepdims=True)
            tops[b] = top
            totals[b], sums[b] = weigh(scores, top, qkv[near, pl.ds(2 * HD, HD)])

    for t in range(1, n - 1):
        for k in range(CHUNKS):
            each_at(t, lambda b, side: pass_on(b, side, k))
            each_at(t - 1, lambda b, side: across(b, k))
            if t == 1 and 1 <= k <= 3:
                for j in range(1, n):
                    w_arrival(j, k - 1).wait_recv()
                    y_copy(j, k - 1).start()

    for k in range(CHUNKS):
        each_at(n - 1, lambda b, side: pass_on(b, side, k))
        if k == 0:
            for copy in own_copies:
                copy.wait()
            for j in range(1, n):
                for i in range(3):
                    y_arrival(j, i).wait_recv()
        if k < 2:
            @pl.loop(k * (CHUNKS // 2), (k + 1) * (CHUNKS // 2))
            def _(kk):
                each_at(n - 2, lambda b, side: across(b, kk))
        if k < n - 1:
            project(k)
        if k == 3:
            pl.loop(0, 2)(attend_near)
        if k == 4:
            attend_near(2)

    @pl.loop(0, CHUNKS)
    def _(k):
        each_at(n - 1, lambda b, side: across(b, k))

    project(n - 1)

    def o_copy(b):
        j = lax.rem(b - s + n, n)
        return remote(
            heads_out.at[b], out.at[:, pl.ds(pl.multiple_of(s * HD, HD), HD)],
            o_send.at[j - 1], o_recv.at[j - 1], seq=b,
        )

    def o_arrival(j):
        owner = lax.rem(s + n - j, n)
        here = out.at[:, pl.ds(pl.multiple_of(owner * HD, HD), HD)]
        return remote(heads_out.at[owner], here, o_send.at[j - 1], o_recv.at[j - 1], seq=owner)

    def give(b, summed, total):
        heads_out[b] = (summed / total).astype(jnp.bfloat16)
        pl.when(b != s)(lambda: o_copy(b).start())

    @pl.loop(1, jnp.where(at_end, 2, n + 1))
    def _(j):
        b = jnp.where(at_end, far, lax.rem(s + j, n))
        scores = scores_of(of_block(b, 0), qkv[:, pl.ds(HD, HD)])
        top = jnp.max(scores, axis=-1, keepdims=True)
        total, summed = weigh(scores, top, qkv[:, pl.ds(2 * HD, HD)])
        give(b, summed, total)

    @pl.when(at_end)
    def _():
        @pl.loop(0, n - 1)
        def _(i):
            b = jnp.where(s == 0, n - 2 - i, 1 + i)
            scores = scores_of(of_block(b, 0), of_block(far, 1))
            top = jnp.maximum(tops[b], jnp.max(scores, axis=-1, keepdims=True))
            total, summed = weigh(scores, top, of_block(far, 2))
            shrink = jnp.exp2((tops[b] - top) * rate)
            give(b, sums[b] * shrink + summed, totals[b] * shrink + total)

    own_out = pltpu.make_async_copy(
        heads_out.at[s], out.at[:, pl.ds(pl.multiple_of(s * HD, HD), HD)], local_sem.at[0]
    )
    own_out.start()

    for j in range(1, n):
        for i in range(3):
            w_copy(j, i).wait_send()
            y_copy(j, i).wait_send()

    @pl.loop(0, n)
    def _(b):
        @pl.loop(0, CHUNKS)
        def _(k):
            pl.when((s < n - 1) & (b <= s))(lambda: up_copy(b, k).wait_send())
            pl.when((s > 0) & (b >= s))(lambda: down_copy(b, k).wait_send())
            x_copy(b, k).wait_send()
            c_copy(b, k, 0).wait_send()
            c_copy(b, k, 1).wait_send()

    own_out.wait()
    for j in range(1, n):
        o_copy(lax.rem(s + j, n)).wait_send()
        o_arrival(j).wait_recv()


def one_head_per_device(acts, w_query, w_key, w_value):
    n = lax.axis_size("seq")
    rows, half_width = acts.shape
    depth, width = w_query.shape
    tokens = n * 2 * rows
    dma = pltpu.SemaphoreType.DMA
    flops = 2 * tokens * depth * n * 3 * HD + 4 * tokens * tokens * HD
    return pl.pallas_call(
        functools.partial(head_kernel, n),
        out_shape=jax.ShapeDtypeStruct((2 * rows, width), jnp.bfloat16),
        in_specs=[pl.BlockSpec(memory_space=pl.ANY)] * 4,
        out_specs=pl.BlockSpec(memory_space=pl.ANY),
        scratch_shapes=[
            pltpu.VMEM((n, 2, 2 * rows, half_width), jnp.bfloat16),
            pltpu.VMEM((n * depth, 3 * HD), jnp.bfloat16),
            pltpu.VMEM((tokens, 3 * HD), jnp.bfloat16),
            pltpu.VMEM((n, 2 * rows, HD), jnp.bfloat16),
            pltpu.VMEM((n, 2 * rows, 1), jnp.float32),
            pltpu.VMEM((n, 2 * rows, 1), jnp.float32),
            pltpu.VMEM((n, 2 * rows, HD), jnp.float32),
            dma((4,)),
            dma((n - 1, 3)), dma((n - 1, 3)), dma((n - 1, 3)), dma((n - 1, 3)),
            dma((n, CHUNKS)), dma((n, CHUNKS)), dma((n, CHUNKS)),
            dma((n, CHUNKS)), dma((n, CHUNKS)),
            dma((2, n, CHUNKS)), dma((2, n, CHUNKS)),
            dma((n - 1,)), dma((n - 1,)),
        ],
        compiler_params=pltpu.CompilerParams(
            collective_id=0, has_side_effects=True, vmem_limit_bytes=63 * 1024 * 1024
        ),
        cost_estimate=pl.CostEstimate(flops=flops, bytes_accessed=2 * tokens * half_width, transcendentals=tokens * tokens),
    )(acts, w_query, w_key, w_value)


def passed_along(block, axis, distance):
    devices = range(lax.axis_size(axis))
    route = [((i - distance) % len(devices), i) for i in devices]
    return lax.ppermute(block, axis, route)


def blocks_passed_along(acts, w_query, w_key, w_value):
    block = lax.all_gather(acts, "row", axis=0, tiled=True)
    block = lax.all_gather(block, "col", axis=1, tiled=True)
    tokens_here = block.shape[0]
    width = w_query.shape[1]
    heads_here = width // HD
    pieces = (
        lax.all_gather(w_query, "seq", axis=0, tiled=True),
        lax.all_gather(w_key, "seq", axis=0, tiled=True),
        lax.all_gather(w_value, "seq", axis=0, tiled=True),
    )
    query_sum, key_sum, value_sum = tuple(
        (jnp.dot(block, piece, preferred_element_type=jnp.float32) for piece in pieces)
    )
    query = query_sum.astype(jnp.bfloat16).reshape(tokens_here, heads_here, HD)
    packed = jnp.stack([key_sum.astype(jnp.bfloat16), value_sum.astype(jnp.bfloat16)])
    blocks_seen = [packed]
    current = packed
    for step in range(1, SPAN):
        current = passed_along(current, "seq", 1)
        blocks_seen.append(current)
    scale = 1.0 / jnp.sqrt(jnp.float32(HD))
    score_list = []
    for seen in blocks_seen:
        seen_keys = seen[0].reshape(-1, heads_here, HD)
        score_list.append(
            jnp.einsum("qhd,khd->hqk", query, seen_keys, preferred_element_type=jnp.float32) * scale
        )
    largest = score_list[0].max(axis=-1, keepdims=True)
    for scores in score_list[1:]:
        largest = jnp.maximum(largest, scores.max(axis=-1, keepdims=True))
    running_total = jnp.zeros((heads_here, tokens_here), jnp.float32)
    summed = jnp.zeros((tokens_here, heads_here, HD), jnp.float32)
    for scores, seen in zip(score_list, blocks_seen):
        expos = jnp.exp(scores - largest)
        running_total = running_total + jnp.sum(expos, axis=-1)
        seen_values = seen[1].reshape(-1, heads_here, HD)
        summed = summed + jnp.einsum(
            "hqk,khd->qhd",
            expos.astype(jnp.bfloat16),
            seen_values,
            preferred_element_type=jnp.float32,
        )
    attended = summed / jnp.transpose(running_total)[:, :, None]
    return attended.astype(jnp.bfloat16).reshape(tokens_here, width)


def per_device(acts, w_query, w_key, w_value):
    n = lax.axis_size("seq")
    pairs = all(lax.axis_size(axis) == 2 for axis in ("groups", "row", "col"))
    depth, width = w_query.shape
    if pairs and n == SPAN and width == n * HD and acts.shape[0] % (16 * CHUNKS) == 0 and depth % 32 == 0:
        return one_head_per_device(acts, w_query, w_key, w_value)
    return blocks_passed_along(acts, w_query, w_key, w_value)


def solution(mesh):
    in_specs = (
        P(("groups", "seq", "row"), "col"),
        P("seq", ("row", "col")),
        P("seq", ("row", "col")),
        P("seq", ("row", "col")),
    )
    out_specs = P(("groups", "seq"), ("row", "col"))
    return jax.shard_map(
        per_device, mesh=mesh, in_specs=in_specs, out_specs=out_specs, check_vma=False
    )
```

```python
import functools
import math

import jax
import jax.numpy as jnp
from jax import lax
from jax.experimental import pallas as pl
from jax.experimental.pallas import tpu as pltpu
from jax.sharding import PartitionSpec as P

HD = 128
SPAN = 4
CHUNKS = 6
MESH = pl.DeviceIdType.MESH


def head_kernel(
    n, acts, w_query, w_key, w_value, out,
    x_all, w_all, given, qkv, heads_out,
    local_sem, w_send, w_recv, y_send, y_recv, xw_send, xw_recv,
    up_send, down_send, z_recv, c_send, c_recv, q_send, q_recv, o_send, o_recv,
):
    g, s = lax.axis_index("groups"), lax.axis_index("seq")
    r, c = lax.axis_index("row"), lax.axis_index("col")
    weights = (w_query, w_key, w_value)
    rows, half_width = acts.shape
    depth = w_query.shape[0]
    half = depth // 2
    part = rows // CHUNKS
    mine, other = pl.ds(0, 3 * HD), pl.ds(3 * HD, 3 * HD)

    barrier = pltpu.get_barrier_semaphore()
    for j in range(1, n):
        pl.semaphore_signal(barrier, inc=1, device_id={"seq": lax.rem(s + j, n)}, device_id_type=MESH)
    pl.semaphore_signal(barrier, inc=1, device_id={"groups": 1 - g}, device_id_type=MESH)
    pl.semaphore_signal(barrier, inc=1, device_id={"row": 1 - r}, device_id_type=MESH)
    pl.semaphore_signal(barrier, inc=1, device_id={"col": 1 - c}, device_id_type=MESH)
    pl.semaphore_wait(barrier, n + 2)

    def remote(src, dst, send, recv, **device):
        return pltpu.make_async_remote_copy(
            src_ref=src, dst_ref=dst, send_sem=send, recv_sem=recv, device_id=device, device_id_type=MESH
        )

    def w_rows(j, which):
        owner = lax.rem(s + n - j, n)
        return pl.ds(pl.multiple_of(owner * depth + which * half, half), half)

    def w_copy(j, i):
        dest = lax.rem(s + j, n)
        return remote(
            weights[i].at[pl.ds(pl.multiple_of(g * half, half), half), pl.ds(pl.multiple_of(dest * HD, HD), HD)],
            w_all.at[w_rows(0, g), pl.ds(i * HD, HD)],
            w_send.at[j - 1, i], w_recv.at[j - 1, i], seq=dest,
        )

    def w_arrival(j, i):
        here = w_all.at[w_rows(j, g), pl.ds(i * HD, HD)]
        return remote(here, here, w_send.at[j - 1, i], w_recv.at[j - 1, i], seq=lax.rem(s + j, n))

    def y_copy(j, whose, which=g):
        here = w_all.at[w_rows(j, which), (mine, other)[whose]]
        return remote(here, here, y_send.at[j - 1, whose], y_recv.at[j - 1, whose], groups=1 - g)

    def y_arrival(j, whose):
        return y_copy(j, whose, 1 - g)

    def xw_copy(j):
        span = w_rows(j, g) if j else pl.ds(pl.multiple_of(s * depth, depth), depth)
        return remote(w_all.at[span, mine], w_all.at[span, other], xw_send.at[j], xw_recv.at[j], row=1 - r)

    def xw_arrival(j):
        span = w_rows(j, g) if j else pl.ds(pl.multiple_of(s * depth, depth), depth)
        here = w_all.at[span, other]
        return remote(here, here, xw_send.at[j], xw_recv.at[j], row=1 - r)

    def spot(b, cc, k):
        return x_all.at[cc, pl.ds(pl.multiple_of(b * rows + k * part, part), part), :]

    def source(b, k, own):
        return acts.at[pl.ds(pl.multiple_of(k * part, part), part), :] if own else spot(b, c, k)

    def up_copy(b, k, own=False):
        return remote(source(b, k, own), spot(b, c, k), up_send.at[b, k], z_recv.at[b, k], seq=s + 1)

    def down_copy(b, k, own=False):
        return remote(source(b, k, own), spot(b, c, k), down_send.at[b, k], z_recv.at[b, k], seq=s - 1)

    def c_copy(b, k, own=False):
        return remote(source(b, k, own), spot(b, c, k), c_send.at[b, k], c_recv.at[b, k], col=1 - c)

    def c_arrival(b, k):
        here = spot(b, 1 - c, k)
        return remote(here, here, c_send.at[b, k], c_recv.at[b, k], col=1 - c)

    own_copies = [
        pltpu.make_async_copy(
            weights[i].at[:, pl.ds(pl.multiple_of(s * HD, HD), HD)],
            w_all.at[pl.ds(pl.multiple_of(s * depth, depth), depth), pl.ds(i * HD, HD)],
            local_sem.at[i],
        )
        for i in range(3)
    ]
    for copy in own_copies:
        copy.start()
    for i in range(3):
        for j in range(1, n):
            w_copy(j, i).start()

    @pl.loop(0, CHUNKS)
    def _(k):
        pl.when(s < n - 1)(lambda: up_copy(s, k, True).start())
        pl.when(s > 0)(lambda: down_copy(s, k, True).start())
        c_copy(s, k, True).start()

    own_acts = pltpu.make_async_copy(
        acts, x_all.at[c, pl.ds(pl.multiple_of(s * rows, rows), rows), :], local_sem.at[3]
    )
    own_acts.start()
    for copy in own_copies:
        copy.wait()
    xw_copy(0).start()

    def each_at(t, body):
        pl.when(s - t >= 0)(lambda: body(s - t, 1))
        pl.when(s + t < n)(lambda: body(s + t, -1))

    def pass_on(b, side, k):
        here = spot(b, c, k)
        remote(here, here, up_send.at[b, k], z_recv.at[b, k], col=1 - c).wait_recv()
        if side > 0:
            pl.when(s < n - 1)(lambda: up_copy(b, k).start())
        else:
            pl.when(s > 0)(lambda: down_copy(b, k).start())
        c_copy(b, k).start()

    low = s < n // 2
    near = pl.multiple_of(jnp.where(low, 0, rows), rows)
    far = pl.multiple_of(jnp.where(low, (n - 1) * rows, 0), rows)
    home = pl.multiple_of(r * n * rows, rows)

    def q_copy(start, size, which):
        return remote(
            given.at[pl.ds(start, size), :], qkv.at[pl.ds(pl.multiple_of(home + start, rows), size), :],
            q_send.at[which], q_recv.at[which], row=1 - r,
        )

    def q_arrival(start, size, which):
        there = pl.multiple_of((1 - r) * n * rows + start, rows)
        return remote(
            given.at[pl.ds(start, size), :], qkv.at[pl.ds(there, size), :], q_send.at[which], q_recv.at[which], row=1 - r
        )

    def project(start, size, which):
        @pl.loop(0, size // rows)
        def _(i):
            @pl.loop(0, CHUNKS)
            def _(k):
                c_arrival(start // rows + i, k).wait_recv()

        span = pl.ds(start, size)
        total = jnp.dot(x_all[0, span, :], w_all[:half_width, :], preferred_element_type=jnp.float32)
        total += jnp.dot(x_all[1, span, :], w_all[half_width:, :], preferred_element_type=jnp.float32)
        given[span, :] = total[:, 3 * HD:].astype(jnp.bfloat16)
        q_copy(start, size, which).start()
        qkv[pl.ds(pl.multiple_of(home + start, rows), size), :] = total[:, :3 * HD].astype(jnp.bfloat16)

    for t in range(1, n):
        for k in range(CHUNKS):
            each_at(t, lambda b, side: pass_on(b, side, k))
            if t == 1 and 1 <= k < n:
                for i in range(3):
                    w_arrival(k, i).wait_recv()
                y_copy(k, 0).start()
                xw_copy(k).start()
            if t == 2 and 1 <= k < n:
                xw_arrival(k).wait_recv()
                y_copy(k, 1).start()
            if t == n - 1 and k == CHUNKS - 2:
                own_acts.wait()
                xw_arrival(0).wait_recv()
                for j in range(1, n):
                    y_arrival(j, 0).wait_recv()
                    y_arrival(j, 1).wait_recv()
                project(near, (n - 1) * rows, 0)
    project(far, rows, 1)
    q_arrival(near, (n - 1) * rows, 0).wait_recv()
    q_arrival(far, rows, 1).wait_recv()

    rate = math.log2(math.e) / math.sqrt(HD)

    def o_copy(j):
        dest = lax.rem(s + j, n)
        return remote(
            heads_out.at[dest], out.at[:, pl.ds(pl.multiple_of(s * HD, HD), HD)],
            o_send.at[j - 1], o_recv.at[j - 1], seq=dest,
        )

    def o_arrival(j):
        owner = lax.rem(s + n - j, n)
        here = out.at[:, pl.ds(pl.multiple_of(owner * HD, HD), HD)]
        return remote(heads_out.at[owner], here, o_send.at[j - 1], o_recv.at[j - 1], seq=owner)

    @pl.loop(1, n + 1)
    def _(j):
        b = lax.rem(s + j, n)
        query = jnp.concatenate([
            qkv[pl.ds(pl.multiple_of((rr * n + b) * rows, rows), rows), pl.ds(0, HD)] for rr in range(2)
        ])
        keys = qkv[:, pl.ds(HD, HD)]
        values = qkv[:, pl.ds(2 * HD, HD)]
        scores = lax.dot_general(
            query, keys, (((1,), (1,)), ((), ())), preferred_element_type=jnp.float32
        )
        expos = jnp.exp2((scores - jnp.max(scores, axis=-1, keepdims=True)) * rate)
        total = jnp.sum(expos, axis=-1, keepdims=True)
        summed = jnp.dot(expos.astype(jnp.bfloat16), values, preferred_element_type=jnp.float32)
        heads_out[b] = (summed / total).astype(jnp.bfloat16)
        pl.when(j < n)(lambda: o_copy(j).start())

    own_out = pltpu.make_async_copy(
        heads_out.at[s], out.at[:, pl.ds(pl.multiple_of(s * HD, HD), HD)], local_sem.at[0]
    )
    own_out.start()

    xw_copy(0).wait_send()
    for j in range(1, n):
        for i in range(3):
            w_copy(j, i).wait_send()
        y_copy(j, 0).wait_send()
        y_copy(j, 1).wait_send()
        xw_copy(j).wait_send()

    @pl.loop(0, n)
    def _(b):
        @pl.loop(0, CHUNKS)
        def _(k):
            pl.when((s < n - 1) & (b <= s))(lambda: up_copy(b, k).wait_send())
            pl.when((s > 0) & (b >= s))(lambda: down_copy(b, k).wait_send())
            c_copy(b, k).wait_send()

    q_copy(near, (n - 1) * rows, 0).wait_send()
    q_copy(far, rows, 1).wait_send()
    own_out.wait()
    for j in range(1, n):
        o_copy(j).wait_send()
        o_arrival(j).wait_recv()


def one_head_per_device(acts, w_query, w_key, w_value):
    n = lax.axis_size("seq")
    rows, half_width = acts.shape
    depth, width = w_query.shape
    tokens = n * 2 * rows
    dma = pltpu.SemaphoreType.DMA
    anywhere = pl.BlockSpec(memory_space=pl.ANY)
    flops = 2 * tokens * depth * n * 3 * HD + 4 * tokens * tokens * HD
    return pl.pallas_call(
        functools.partial(head_kernel, n),
        out_shape=jax.ShapeDtypeStruct((2 * rows, width), jnp.bfloat16),
        in_specs=[anywhere] * 4,
        out_specs=anywhere,
        scratch_shapes=[
            pltpu.VMEM((2, n * rows, half_width), jnp.bfloat16),
            pltpu.VMEM((n * depth, 6 * HD), jnp.bfloat16),
            pltpu.VMEM((n * rows, 3 * HD), jnp.bfloat16),
            pltpu.VMEM((tokens, 3 * HD), jnp.bfloat16),
            pltpu.VMEM((n, 2 * rows, HD), jnp.bfloat16),
            dma((4,)),
            dma((n - 1, 3)), dma((n - 1, 3)), dma((n - 1, 2)), dma((n - 1, 2)), dma((n,)), dma((n,)),
            dma((n, CHUNKS)), dma((n, CHUNKS)), dma((n, CHUNKS)), dma((n, CHUNKS)), dma((n, CHUNKS)),
            dma((2,)), dma((2,)),
            dma((n - 1,)), dma((n - 1,)),
        ],
        compiler_params=pltpu.CompilerParams(
            collective_id=0, has_side_effects=True, vmem_limit_bytes=63 * 1024 * 1024
        ),
        cost_estimate=pl.CostEstimate(flops=flops, bytes_accessed=2 * tokens * half_width, transcendentals=tokens * tokens),
    )(acts, w_query, w_key, w_value)


def passed_along(block, axis, distance):
    devices = range(lax.axis_size(axis))
    route = [((i - distance) % len(devices), i) for i in devices]
    return lax.ppermute(block, axis, route)


def blocks_passed_along(acts, w_query, w_key, w_value):
    block = lax.all_gather(acts, "row", axis=0, tiled=True)
    block = lax.all_gather(block, "col", axis=1, tiled=True)
    tokens_here = block.shape[0]
    width = w_query.shape[1]
    heads_here = width // HD
    pieces = (
        lax.all_gather(w_query, "seq", axis=0, tiled=True),
        lax.all_gather(w_key, "seq", axis=0, tiled=True),
        lax.all_gather(w_value, "seq", axis=0, tiled=True),
    )
    query_sum, key_sum, value_sum = tuple(
        (jnp.dot(block, piece, preferred_element_type=jnp.float32) for piece in pieces)
    )
    query = query_sum.astype(jnp.bfloat16).reshape(tokens_here, heads_here, HD)
    packed = jnp.stack([key_sum.astype(jnp.bfloat16), value_sum.astype(jnp.bfloat16)])
    blocks_seen = [packed]
    current = packed
    for step in range(1, SPAN):
        current = passed_along(current, "seq", 1)
        blocks_seen.append(current)
    scale = 1.0 / jnp.sqrt(jnp.float32(HD))
    score_list = []
    for seen in blocks_seen:
        seen_keys = seen[0].reshape(-1, heads_here, HD)
        score_list.append(
            jnp.einsum("qhd,khd->hqk", query, seen_keys, preferred_element_type=jnp.float32) * scale
        )
    largest = score_list[0].max(axis=-1, keepdims=True)
    for scores in score_list[1:]:
        largest = jnp.maximum(largest, scores.max(axis=-1, keepdims=True))
    running_total = jnp.zeros((heads_here, tokens_here), jnp.float32)
    summed = jnp.zeros((tokens_here, heads_here, HD), jnp.float32)
    for scores, seen in zip(score_list, blocks_seen):
        expos = jnp.exp(scores - largest)
        running_total = running_total + jnp.sum(expos, axis=-1)
        seen_values = seen[1].reshape(-1, heads_here, HD)
        summed = summed + jnp.einsum(
            "hqk,khd->qhd",
            expos.astype(jnp.bfloat16),
            seen_values,
            preferred_element_type=jnp.float32,
        )
    attended = summed / jnp.transpose(running_total)[:, :, None]
    return attended.astype(jnp.bfloat16).reshape(tokens_here, width)


def per_device(acts, w_query, w_key, w_value):
    n = lax.axis_size("seq")
    pairs = all(lax.axis_size(axis) == 2 for axis in ("groups", "row", "col"))
    depth, width = w_query.shape
    if pairs and n == SPAN and width == n * HD and acts.shape[0] % (16 * CHUNKS) == 0 and depth % 32 == 0:
        return one_head_per_device(acts, w_query, w_key, w_value)
    return blocks_passed_along(acts, w_query, w_key, w_value)


def solution(mesh):
    in_specs = (
        P(("groups", "seq", "row"), "col"),
        P("seq", ("row", "col")),
        P("seq", ("row", "col")),
        P("seq", ("row", "col")),
    )
    out_specs = P(("groups", "seq"), ("row", "col"))
    return jax.shard_map(
        per_device, mesh=mesh, in_specs=in_specs, out_specs=out_specs, check_vma=False
    )
```

```python
import functools
import math

import jax
import jax.numpy as jnp
from jax import lax
from jax.experimental import pallas as pl
from jax.experimental.pallas import tpu as pltpu
from jax.sharding import PartitionSpec as P

HD = 128
SPAN = 4
CHUNKS = 6
MESH = pl.DeviceIdType.MESH


def head_kernel(
    n, acts, w_query, w_key, w_value, out,
    x_all, w_all, qkv, heads_out,
    local_sem, w_send, w_recv, y_send, y_recv,
    up_send, down_send, z_recv, x_send, x_recv, c_send, c_recv, o_send, o_recv,
):
    g, s = lax.axis_index("groups"), lax.axis_index("seq")
    r, c = lax.axis_index("row"), lax.axis_index("col")
    weights = (w_query, w_key, w_value)
    rows, half_width = acts.shape
    depth = w_query.shape[0]
    half = depth // 2
    block = 2 * rows
    part = rows // CHUNKS

    barrier = pltpu.get_barrier_semaphore()
    for j in range(1, n):
        pl.semaphore_signal(barrier, inc=1, device_id={"seq": lax.rem(s + j, n)}, device_id_type=MESH)
    pl.semaphore_signal(barrier, inc=1, device_id={"groups": 1 - g}, device_id_type=MESH)
    pl.semaphore_signal(barrier, inc=1, device_id={"row": 1 - r}, device_id_type=MESH)
    pl.semaphore_signal(barrier, inc=1, device_id={"col": 1 - c}, device_id_type=MESH)
    pl.semaphore_wait(barrier, n + 2)

    def remote(src, dst, send, recv, **device):
        return pltpu.make_async_remote_copy(
            src_ref=src, dst_ref=dst, send_sem=send, recv_sem=recv, device_id=device, device_id_type=MESH
        )

    def w_rows(owner, which):
        return pl.ds(pl.multiple_of(owner * depth + which * half, half), half)

    def w_copy(j, i):
        dest = lax.rem(s + j, n)
        return remote(
            weights[i].at[pl.ds(pl.multiple_of(g * half, half), half), pl.ds(pl.multiple_of(dest * HD, HD), HD)],
            w_all.at[w_rows(s, g), pl.ds(i * HD, HD)],
            w_send.at[j - 1, i], w_recv.at[j - 1, i], seq=dest,
        )

    def w_arrival(j, i):
        owner = lax.rem(s + n - j, n)
        here = w_all.at[w_rows(owner, g), pl.ds(i * HD, HD)]
        return remote(here, here, w_send.at[j - 1, i], w_recv.at[j - 1, i], seq=lax.rem(s + j, n))

    def y_copy(j, i, which=g):
        owner = lax.rem(s + n - j, n)
        here = w_all.at[w_rows(owner, which), pl.ds(i * HD, HD)]
        return remote(here, here, y_send.at[j - 1, i], y_recv.at[j - 1, i], groups=1 - g)

    def y_arrival(j, i):
        return y_copy(j, i, 1 - g)

    def spot(b, rr, cc, k):
        return x_all.at[b, cc, pl.ds(pl.multiple_of(rr * rows + k * part, part), part), :]

    def source(b, k, own):
        return acts.at[pl.ds(pl.multiple_of(k * part, part), part), :] if own else spot(b, r, c, k)

    def up_copy(b, k, own=False):
        return remote(source(b, k, own), spot(b, r, c, k), up_send.at[b, k], z_recv.at[b, k], seq=s + 1)

    def down_copy(b, k, own=False):
        return remote(source(b, k, own), spot(b, r, c, k), down_send.at[b, k], z_recv.at[b, k], seq=s - 1)

    def x_copy(b, k, own=False):
        return remote(source(b, k, own), spot(b, r, c, k), x_send.at[b, k], x_recv.at[b, k], row=1 - r)

    def x_arrival(b, k):
        here = spot(b, 1 - r, c, k)
        return remote(here, here, x_send.at[b, k], x_recv.at[b, k], row=1 - r)

    def c_copy(b, k, rr, own=False):
        src = source(b, k, True) if own else spot(b, rr, c, k)
        return remote(src, spot(b, rr, c, k), c_send.at[rr, b, k], c_recv.at[rr, b, k], col=1 - c)

    def c_arrival(b, k, rr):
        here = spot(b, rr, 1 - c, k)
        return remote(here, here, c_send.at[rr, b, k], c_recv.at[rr, b, k], col=1 - c)

    for i in range(3):
        for j in range(1, n):
            w_copy(j, i).start()

    @pl.loop(0, CHUNKS)
    def _(k):
        @pl.when(s < n - 1)
        def _():
            up_copy(s, k, True).start()

        @pl.when(s > 0)
        def _():
            down_copy(s, k, True).start()

        x_copy(s, k, True).start()
        c_copy(s, k, r, True).start()

    own_copies = [
        pltpu.make_async_copy(
            acts, x_all.at[s, c, pl.ds(pl.multiple_of(r * rows, rows), rows), :], local_sem.at[0]
        )
    ] + [
        pltpu.make_async_copy(
            weights[i].at[:, pl.ds(pl.multiple_of(s * HD, HD), HD)],
            w_all.at[pl.ds(pl.multiple_of(s * depth, depth), depth), pl.ds(i * HD, HD)],
            local_sem.at[1 + i],
        )
        for i in range(3)
    ]
    for copy in own_copies:
        copy.start()

    def each_at(t, body):
        if t == 0:
            body(s, 0)
            return
        pl.when(s - t >= 0)(lambda: body(s - t, 1))
        pl.when(s + t < n)(lambda: body(s + t, -1))

    def pass_on(b, side, k):
        here = spot(b, r, c, k)
        remote(here, here, up_send.at[b, k], z_recv.at[b, k], row=1 - r).wait_recv()
        if side > 0:
            pl.when(s < n - 1)(lambda: up_copy(b, k).start())
        else:
            pl.when(s > 0)(lambda: down_copy(b, k).start())
        x_copy(b, k).start()
        c_copy(b, k, r).start()

    def across(b, k):
        x_arrival(b, k).wait_recv()
        c_copy(b, k, 1 - r).start()

    def project(t):
        @pl.loop(0, 2 if t else 1)
        def _(side):
            b = s + (2 * side - 1) * t

            @pl.when((b >= 0) & (b < n))
            def _():
                @pl.loop(0, CHUNKS)
                def _(k):
                    c_arrival(b, k, 0).wait_recv()
                    c_arrival(b, k, 1).wait_recv()

                total = jnp.dot(x_all[b, 0], w_all[:half_width, :], preferred_element_type=jnp.float32)
                total += jnp.dot(x_all[b, 1], w_all[half_width:, :], preferred_element_type=jnp.float32)
                qkv[pl.ds(pl.multiple_of(b * block, block), block), :] = total.astype(jnp.bfloat16)

    for t in range(1, n):
        for k in range(CHUNKS):
            each_at(t, lambda b, side: pass_on(b, side, k))
            each_at(t - 1, lambda b, side: across(b, k))
            if t == 2 and 1 <= k <= 3:
                for j in range(1, n):
                    w_arrival(j, k - 1).wait_recv()
                    y_copy(j, k - 1).start()
            if t == n - 1 and k == 3:
                for copy in own_copies:
                    copy.wait()
                for j in range(1, n):
                    for i in range(3):
                        y_arrival(j, i).wait_recv()
            if t == n - 1 and k >= 3 and k - 3 < n - 2:
                project(k - 3)
    project(n - 2)

    @pl.loop(0, CHUNKS)
    def _(k):
        each_at(n - 1, lambda b, side: across(b, k))

    project(n - 1)

    rate = math.log2(math.e) / math.sqrt(HD)

    def o_copy(j):
        dest = lax.rem(s + j, n)
        return remote(
            heads_out.at[dest], out.at[:, pl.ds(pl.multiple_of(s * HD, HD), HD)],
            o_send.at[j - 1], o_recv.at[j - 1], seq=dest,
        )

    def o_arrival(j):
        owner = lax.rem(s + n - j, n)
        here = out.at[:, pl.ds(pl.multiple_of(owner * HD, HD), HD)]
        return remote(heads_out.at[owner], here, o_send.at[j - 1], o_recv.at[j - 1], seq=owner)

    @pl.loop(1, n + 1)
    def _(j):
        b = lax.rem(s + j, n)
        query = qkv[pl.ds(pl.multiple_of(b * block, block), block), pl.ds(0, HD)]
        keys = qkv[:, pl.ds(HD, HD)]
        values = qkv[:, pl.ds(2 * HD, HD)]
        scores = lax.dot_general(
            query, keys, (((1,), (1,)), ((), ())), preferred_element_type=jnp.float32
        )
        expos = jnp.exp2((scores - jnp.max(scores, axis=-1, keepdims=True)) * rate)
        total = jnp.sum(expos, axis=-1, keepdims=True)
        summed = jnp.dot(expos.astype(jnp.bfloat16), values, preferred_element_type=jnp.float32)
        heads_out[b] = (summed / total).astype(jnp.bfloat16)
        pl.when(j < n)(lambda: o_copy(j).start())

    own_out = pltpu.make_async_copy(
        heads_out.at[s], out.at[:, pl.ds(pl.multiple_of(s * HD, HD), HD)], local_sem.at[0]
    )
    own_out.start()

    for j in range(1, n):
        for i in range(3):
            w_copy(j, i).wait_send()
            y_copy(j, i).wait_send()

    @pl.loop(0, n)
    def _(b):
        @pl.loop(0, CHUNKS)
        def _(k):
            pl.when((s < n - 1) & (b <= s))(lambda: up_copy(b, k).wait_send())
            pl.when((s > 0) & (b >= s))(lambda: down_copy(b, k).wait_send())
            x_copy(b, k).wait_send()
            c_copy(b, k, 0).wait_send()
            c_copy(b, k, 1).wait_send()

    own_out.wait()
    for j in range(1, n):
        o_copy(j).wait_send()
        o_arrival(j).wait_recv()


def one_head_per_device(acts, w_query, w_key, w_value):
    n = lax.axis_size("seq")
    rows, half_width = acts.shape
    depth, width = w_query.shape
    tokens = n * 2 * rows
    dma = pltpu.SemaphoreType.DMA
    flops = 2 * tokens * depth * n * 3 * HD + 4 * tokens * tokens * HD
    return pl.pallas_call(
        functools.partial(head_kernel, n),
        out_shape=jax.ShapeDtypeStruct((2 * rows, width), jnp.bfloat16),
        in_specs=[pl.BlockSpec(memory_space=pl.ANY)] * 4,
        out_specs=pl.BlockSpec(memory_space=pl.ANY),
        scratch_shapes=[
            pltpu.VMEM((n, 2, 2 * rows, half_width), jnp.bfloat16),
            pltpu.VMEM((n * depth, 3 * HD), jnp.bfloat16),
            pltpu.VMEM((tokens, 3 * HD), jnp.bfloat16),
            pltpu.VMEM((n, 2 * rows, HD), jnp.bfloat16),
            dma((4,)),
            dma((n - 1, 3)), dma((n - 1, 3)), dma((n - 1, 3)), dma((n - 1, 3)),
            dma((n, CHUNKS)), dma((n, CHUNKS)), dma((n, CHUNKS)),
            dma((n, CHUNKS)), dma((n, CHUNKS)),
            dma((2, n, CHUNKS)), dma((2, n, CHUNKS)),
            dma((n - 1,)), dma((n - 1,)),
        ],
        compiler_params=pltpu.CompilerParams(
            collective_id=0, has_side_effects=True, vmem_limit_bytes=63 * 1024 * 1024
        ),
        cost_estimate=pl.CostEstimate(flops=flops, bytes_accessed=2 * tokens * half_width, transcendentals=tokens * tokens),
    )(acts, w_query, w_key, w_value)


def passed_along(block, axis, distance):
    devices = range(lax.axis_size(axis))
    route = [((i - distance) % len(devices), i) for i in devices]
    return lax.ppermute(block, axis, route)


def blocks_passed_along(acts, w_query, w_key, w_value):
    block = lax.all_gather(acts, "row", axis=0, tiled=True)
    block = lax.all_gather(block, "col", axis=1, tiled=True)
    tokens_here = block.shape[0]
    width = w_query.shape[1]
    heads_here = width // HD
    pieces = (
        lax.all_gather(w_query, "seq", axis=0, tiled=True),
        lax.all_gather(w_key, "seq", axis=0, tiled=True),
        lax.all_gather(w_value, "seq", axis=0, tiled=True),
    )
    query_sum, key_sum, value_sum = tuple(
        (jnp.dot(block, piece, preferred_element_type=jnp.float32) for piece in pieces)
    )
    query = query_sum.astype(jnp.bfloat16).reshape(tokens_here, heads_here, HD)
    packed = jnp.stack([key_sum.astype(jnp.bfloat16), value_sum.astype(jnp.bfloat16)])
    blocks_seen = [packed]
    current = packed
    for step in range(1, SPAN):
        current = passed_along(current, "seq", 1)
        blocks_seen.append(current)
    scale = 1.0 / jnp.sqrt(jnp.float32(HD))
    score_list = []
    for seen in blocks_seen:
        seen_keys = seen[0].reshape(-1, heads_here, HD)
        score_list.append(
            jnp.einsum("qhd,khd->hqk", query, seen_keys, preferred_element_type=jnp.float32) * scale
        )
    largest = score_list[0].max(axis=-1, keepdims=True)
    for scores in score_list[1:]:
        largest = jnp.maximum(largest, scores.max(axis=-1, keepdims=True))
    running_total = jnp.zeros((heads_here, tokens_here), jnp.float32)
    summed = jnp.zeros((tokens_here, heads_here, HD), jnp.float32)
    for scores, seen in zip(score_list, blocks_seen):
        expos = jnp.exp(scores - largest)
        running_total = running_total + jnp.sum(expos, axis=-1)
        seen_values = seen[1].reshape(-1, heads_here, HD)
        summed = summed + jnp.einsum(
            "hqk,khd->qhd",
            expos.astype(jnp.bfloat16),
            seen_values,
            preferred_element_type=jnp.float32,
        )
    attended = summed / jnp.transpose(running_total)[:, :, None]
    return attended.astype(jnp.bfloat16).reshape(tokens_here, width)


def per_device(acts, w_query, w_key, w_value):
    n = lax.axis_size("seq")
    pairs = all(lax.axis_size(axis) == 2 for axis in ("groups", "row", "col"))
    depth, width = w_query.shape
    if pairs and n == SPAN and width == n * HD and acts.shape[0] % (16 * CHUNKS) == 0 and depth % 32 == 0:
        return one_head_per_device(acts, w_query, w_key, w_value)
    return blocks_passed_along(acts, w_query, w_key, w_value)


def solution(mesh):
    in_specs = (
        P(("groups", "seq", "row"), "col"),
        P("seq", ("row", "col")),
        P("seq", ("row", "col")),
        P("seq", ("row", "col")),
    )
    out_specs = P(("groups", "seq"), ("row", "col"))
    return jax.shard_map(
        per_device, mesh=mesh, in_specs=in_specs, out_specs=out_specs, check_vma=False
    )
```

```python
import functools
import math

import jax
import jax.numpy as jnp
from jax import lax
from jax.experimental import pallas as pl
from jax.experimental.pallas import tpu as pltpu
from jax.sharding import PartitionSpec as P

HD = 128
SPAN = 4
CHUNKS = 6
MESH = pl.DeviceIdType.MESH


def head_kernel(
    n, acts, w_query, w_key, w_value, out,
    x_all, w_all, qkv, heads_out,
    local_sem, w_send, w_recv, y_send, y_recv,
    up_send, down_send, z_recv, x_send, x_recv, c_send, c_recv, o_send, o_recv,
):
    g, s = lax.axis_index("groups"), lax.axis_index("seq")
    r, c = lax.axis_index("row"), lax.axis_index("col")
    weights = (w_query, w_key, w_value)
    rows, half_width = acts.shape
    depth = w_query.shape[0]
    half = depth // 2
    block = 2 * rows
    part = rows // CHUNKS

    barrier = pltpu.get_barrier_semaphore()
    for j in range(1, n):
        pl.semaphore_signal(barrier, inc=1, device_id={"seq": lax.rem(s + j, n)}, device_id_type=MESH)
    pl.semaphore_signal(barrier, inc=1, device_id={"groups": 1 - g}, device_id_type=MESH)
    pl.semaphore_signal(barrier, inc=1, device_id={"row": 1 - r}, device_id_type=MESH)
    pl.semaphore_signal(barrier, inc=1, device_id={"col": 1 - c}, device_id_type=MESH)
    pl.semaphore_wait(barrier, n + 2)

    def remote(src, dst, send, recv, **device):
        return pltpu.make_async_remote_copy(
            src_ref=src, dst_ref=dst, send_sem=send, recv_sem=recv, device_id=device, device_id_type=MESH
        )

    def w_rows(owner, which):
        return pl.ds(pl.multiple_of(owner * depth + which * half, half), half)

    def w_copy(j, i):
        dest = lax.rem(s + j, n)
        return remote(
            weights[i].at[pl.ds(pl.multiple_of(g * half, half), half), pl.ds(pl.multiple_of(dest * HD, HD), HD)],
            w_all.at[w_rows(s, g), pl.ds(i * HD, HD)],
            w_send.at[j - 1, i], w_recv.at[j - 1, i], seq=dest,
        )

    def w_arrival(j, i):
        owner = lax.rem(s + n - j, n)
        here = w_all.at[w_rows(owner, g), pl.ds(i * HD, HD)]
        return remote(here, here, w_send.at[j - 1, i], w_recv.at[j - 1, i], seq=lax.rem(s + j, n))

    def y_copy(j, i, which=g):
        owner = lax.rem(s + n - j, n)
        here = w_all.at[w_rows(owner, which), pl.ds(i * HD, HD)]
        return remote(here, here, y_send.at[j - 1, i], y_recv.at[j - 1, i], groups=1 - g)

    def y_arrival(j, i):
        return y_copy(j, i, 1 - g)

    def spot(b, rr, cc, k):
        return x_all.at[b, cc, pl.ds(pl.multiple_of(rr * rows + k * part, part), part), :]

    def source(b, k, own):
        return acts.at[pl.ds(pl.multiple_of(k * part, part), part), :] if own else spot(b, r, c, k)

    def up_copy(b, k, own=False):
        return remote(source(b, k, own), spot(b, r, c, k), up_send.at[b, k], z_recv.at[b, k], seq=s + 1)

    def down_copy(b, k, own=False):
        return remote(source(b, k, own), spot(b, r, c, k), down_send.at[b, k], z_recv.at[b, k], seq=s - 1)

    def x_copy(b, k, own=False):
        return remote(source(b, k, own), spot(b, r, c, k), x_send.at[b, k], x_recv.at[b, k], row=1 - r)

    def x_arrival(b, k):
        here = spot(b, 1 - r, c, k)
        return remote(here, here, x_send.at[b, k], x_recv.at[b, k], row=1 - r)

    def c_copy(b, k, rr, own=False):
        src = source(b, k, True) if own else spot(b, rr, c, k)
        return remote(src, spot(b, rr, c, k), c_send.at[rr, b, k], c_recv.at[rr, b, k], col=1 - c)

    def c_arrival(b, k, rr):
        here = spot(b, rr, 1 - c, k)
        return remote(here, here, c_send.at[rr, b, k], c_recv.at[rr, b, k], col=1 - c)

    for i in range(3):
        for j in range(1, n):
            w_copy(j, i).start()

    @pl.loop(0, CHUNKS)
    def _(k):
        x_copy(s, k, True).start()
        c_copy(s, k, r, True).start()

    own_copies = [
        pltpu.make_async_copy(
            acts, x_all.at[s, c, pl.ds(pl.multiple_of(r * rows, rows), rows), :], local_sem.at[0]
        )
    ] + [
        pltpu.make_async_copy(
            weights[i].at[:, pl.ds(pl.multiple_of(s * HD, HD), HD)],
            w_all.at[pl.ds(pl.multiple_of(s * depth, depth), depth), pl.ds(i * HD, HD)],
            local_sem.at[1 + i],
        )
        for i in range(3)
    ]
    for copy in own_copies:
        copy.start()

    for i in range(2):
        for j in range(1, n):
            w_copy(j, i).wait_send()

    @pl.loop(0, CHUNKS)
    def _(k):
        pl.when(s < n - 1)(lambda: up_copy(s, k, True).start())
        pl.when(s > 0)(lambda: down_copy(s, k, True).start())

    def weights_on(i):
        for j in range(1, n):
            w_arrival(j, i).wait_recv()
            y_copy(j, i).start()

    def each_at(t, body):
        if t == 0:
            body(s, 0)
            return
        pl.when(s - t >= 0)(lambda: body(s - t, 1))
        pl.when(s + t < n)(lambda: body(s + t, -1))

    def pass_on(b, side, k):
        here = spot(b, r, c, k)
        remote(here, here, up_send.at[b, k], z_recv.at[b, k], row=1 - r).wait_recv()
        if side > 0:
            pl.when(s < n - 1)(lambda: up_copy(b, k).start())
        else:
            pl.when(s > 0)(lambda: down_copy(b, k).start())
        x_copy(b, k).start()
        c_copy(b, k, r).start()

    def across(b, k):
        x_arrival(b, k).wait_recv()
        c_copy(b, k, 1 - r).start()

    def project(t):
        @pl.loop(0, 2 if t else 1)
        def _(side):
            b = s + (2 * side - 1) * t

            @pl.when((b >= 0) & (b < n))
            def _():
                @pl.loop(0, CHUNKS)
                def _(k):
                    c_arrival(b, k, 0).wait_recv()
                    c_arrival(b, k, 1).wait_recv()

                total = jnp.dot(x_all[b, 0], w_all[:half_width, :], preferred_element_type=jnp.float32)
                total += jnp.dot(x_all[b, 1], w_all[half_width:, :], preferred_element_type=jnp.float32)
                qkv[pl.ds(pl.multiple_of(b * block, block), block), :] = total.astype(jnp.bfloat16)

    weights_on(0)
    weights_on(1)
    for t in range(1, n):
        for k in range(CHUNKS):
            each_at(t, lambda b, side: pass_on(b, side, k))
            each_at(t - 1, lambda b, side: across(b, k))
            if t == 1 and k == 1:
                weights_on(2)
            if t == n - 1 and k == 0:
                for copy in own_copies:
                    copy.wait()
                for j in range(1, n):
                    for i in range(3):
                        y_arrival(j, i).wait_recv()
            if t == n - 1 and k < n - 2:
                project(k)
    project(n - 2)

    @pl.loop(0, CHUNKS)
    def _(k):
        each_at(n - 1, lambda b, side: across(b, k))

    project(n - 1)

    rate = math.log2(math.e) / math.sqrt(HD)

    def o_copy(j):
        dest = lax.rem(s + j, n)
        return remote(
            heads_out.at[dest], out.at[:, pl.ds(pl.multiple_of(s * HD, HD), HD)],
            o_send.at[j - 1], o_recv.at[j - 1], seq=dest,
        )

    def o_arrival(j):
        owner = lax.rem(s + n - j, n)
        here = out.at[:, pl.ds(pl.multiple_of(owner * HD, HD), HD)]
        return remote(heads_out.at[owner], here, o_send.at[j - 1], o_recv.at[j - 1], seq=owner)

    @pl.loop(1, n + 1)
    def _(j):
        b = lax.rem(s + j, n)
        query = qkv[pl.ds(pl.multiple_of(b * block, block), block), pl.ds(0, HD)]
        keys = qkv[:, pl.ds(HD, HD)]
        values = qkv[:, pl.ds(2 * HD, HD)]
        scores = lax.dot_general(
            query, keys, (((1,), (1,)), ((), ())), preferred_element_type=jnp.float32
        )
        expos = jnp.exp2((scores - jnp.max(scores, axis=-1, keepdims=True)) * rate)
        total = jnp.sum(expos, axis=-1, keepdims=True)
        summed = jnp.dot(expos.astype(jnp.bfloat16), values, preferred_element_type=jnp.float32)
        heads_out[b] = (summed / total).astype(jnp.bfloat16)
        pl.when(j < n)(lambda: o_copy(j).start())

    own_out = pltpu.make_async_copy(
        heads_out.at[s], out.at[:, pl.ds(pl.multiple_of(s * HD, HD), HD)], local_sem.at[0]
    )
    own_out.start()

    for j in range(1, n):
        w_copy(j, 2).wait_send()
        for i in range(3):
            y_copy(j, i).wait_send()

    @pl.loop(0, n)
    def _(b):
        @pl.loop(0, CHUNKS)
        def _(k):
            pl.when((s < n - 1) & (b <= s))(lambda: up_copy(b, k).wait_send())
            pl.when((s > 0) & (b >= s))(lambda: down_copy(b, k).wait_send())
            x_copy(b, k).wait_send()
            c_copy(b, k, 0).wait_send()
            c_copy(b, k, 1).wait_send()

    own_out.wait()
    for j in range(1, n):
        o_copy(j).wait_send()
        o_arrival(j).wait_recv()


def one_head_per_device(acts, w_query, w_key, w_value):
    n = lax.axis_size("seq")
    rows, half_width = acts.shape
    depth, width = w_query.shape
    tokens = n * 2 * rows
    dma = pltpu.SemaphoreType.DMA
    flops = 2 * tokens * depth * n * 3 * HD + 4 * tokens * tokens * HD
    return pl.pallas_call(
        functools.partial(head_kernel, n),
        out_shape=jax.ShapeDtypeStruct((2 * rows, width), jnp.bfloat16),
        in_specs=[pl.BlockSpec(memory_space=pl.ANY)] * 4,
        out_specs=pl.BlockSpec(memory_space=pl.ANY),
        scratch_shapes=[
            pltpu.VMEM((n, 2, 2 * rows, half_width), jnp.bfloat16),
            pltpu.VMEM((n * depth, 3 * HD), jnp.bfloat16),
            pltpu.VMEM((tokens, 3 * HD), jnp.bfloat16),
            pltpu.VMEM((n, 2 * rows, HD), jnp.bfloat16),
            dma((4,)),
            dma((n - 1, 3)), dma((n - 1, 3)), dma((n - 1, 3)), dma((n - 1, 3)),
            dma((n, CHUNKS)), dma((n, CHUNKS)), dma((n, CHUNKS)),
            dma((n, CHUNKS)), dma((n, CHUNKS)),
            dma((2, n, CHUNKS)), dma((2, n, CHUNKS)),
            dma((n - 1,)), dma((n - 1,)),
        ],
        compiler_params=pltpu.CompilerParams(
            collective_id=0, has_side_effects=True, vmem_limit_bytes=63 * 1024 * 1024
        ),
        cost_estimate=pl.CostEstimate(flops=flops, bytes_accessed=2 * tokens * half_width, transcendentals=tokens * tokens),
    )(acts, w_query, w_key, w_value)


def passed_along(block, axis, distance):
    devices = range(lax.axis_size(axis))
    route = [((i - distance) % len(devices), i) for i in devices]
    return lax.ppermute(block, axis, route)


def blocks_passed_along(acts, w_query, w_key, w_value):
    block = lax.all_gather(acts, "row", axis=0, tiled=True)
    block = lax.all_gather(block, "col", axis=1, tiled=True)
    tokens_here = block.shape[0]
    width = w_query.shape[1]
    heads_here = width // HD
    pieces = (
        lax.all_gather(w_query, "seq", axis=0, tiled=True),
        lax.all_gather(w_key, "seq", axis=0, tiled=True),
        lax.all_gather(w_value, "seq", axis=0, tiled=True),
    )
    query_sum, key_sum, value_sum = tuple(
        (jnp.dot(block, piece, preferred_element_type=jnp.float32) for piece in pieces)
    )
    query = query_sum.astype(jnp.bfloat16).reshape(tokens_here, heads_here, HD)
    packed = jnp.stack([key_sum.astype(jnp.bfloat16), value_sum.astype(jnp.bfloat16)])
    blocks_seen = [packed]
    current = packed
    for step in range(1, SPAN):
        current = passed_along(current, "seq", 1)
        blocks_seen.append(current)
    scale = 1.0 / jnp.sqrt(jnp.float32(HD))
    score_list = []
    for seen in blocks_seen:
        seen_keys = seen[0].reshape(-1, heads_here, HD)
        score_list.append(
            jnp.einsum("qhd,khd->hqk", query, seen_keys, preferred_element_type=jnp.float32) * scale
        )
    largest = score_list[0].max(axis=-1, keepdims=True)
    for scores in score_list[1:]:
        largest = jnp.maximum(largest, scores.max(axis=-1, keepdims=True))
    running_total = jnp.zeros((heads_here, tokens_here), jnp.float32)
    summed = jnp.zeros((tokens_here, heads_here, HD), jnp.float32)
    for scores, seen in zip(score_list, blocks_seen):
        expos = jnp.exp(scores - largest)
        running_total = running_total + jnp.sum(expos, axis=-1)
        seen_values = seen[1].reshape(-1, heads_here, HD)
        summed = summed + jnp.einsum(
            "hqk,khd->qhd",
            expos.astype(jnp.bfloat16),
            seen_values,
            preferred_element_type=jnp.float32,
        )
    attended = summed / jnp.transpose(running_total)[:, :, None]
    return attended.astype(jnp.bfloat16).reshape(tokens_here, width)


def per_device(acts, w_query, w_key, w_value):
    n = lax.axis_size("seq")
    pairs = all(lax.axis_size(axis) == 2 for axis in ("groups", "row", "col"))
    depth, width = w_query.shape
    if pairs and n == SPAN and width == n * HD and acts.shape[0] % (16 * CHUNKS) == 0 and depth % 32 == 0:
        return one_head_per_device(acts, w_query, w_key, w_value)
    return blocks_passed_along(acts, w_query, w_key, w_value)


def solution(mesh):
    in_specs = (
        P(("groups", "seq", "row"), "col"),
        P("seq", ("row", "col")),
        P("seq", ("row", "col")),
        P("seq", ("row", "col")),
    )
    out_specs = P(("groups", "seq"), ("row", "col"))
    return jax.shard_map(
        per_device, mesh=mesh, in_specs=in_specs, out_specs=out_specs, check_vma=False
    )
```

```python
import functools
import math

import jax
import jax.numpy as jnp
from jax import lax
from jax.experimental import pallas as pl
from jax.experimental.pallas import tpu as pltpu
from jax.sharding import PartitionSpec as P

HD = 128
SPAN = 4
CHUNKS = 6
PIECES = 4
MESH = pl.DeviceIdType.MESH


def head_kernel(
    n, acts, w_query, w_key, w_value, out,
    x_all, w_all, packed, qkv, heads_out,
    local_sem, pack_sem, w_send, w_recv, y_send, y_recv,
    up_send, down_send, z_recv, x_send, x_recv, c_send, c_recv, o_send, o_recv,
):
    g, s = lax.axis_index("groups"), lax.axis_index("seq")
    r, c = lax.axis_index("row"), lax.axis_index("col")
    weights = (w_query, w_key, w_value)
    rows, half_width = acts.shape
    depth = w_query.shape[0]
    half = depth // 2
    piece = half // PIECES
    block = 2 * rows
    part = rows // CHUNKS

    barrier = pltpu.get_barrier_semaphore()
    for j in range(1, n):
        pl.semaphore_signal(barrier, inc=1, device_id={"seq": lax.rem(s + j, n)}, device_id_type=MESH)
    pl.semaphore_signal(barrier, inc=1, device_id={"groups": 1 - g}, device_id_type=MESH)
    pl.semaphore_signal(barrier, inc=1, device_id={"row": 1 - r}, device_id_type=MESH)
    pl.semaphore_signal(barrier, inc=1, device_id={"col": 1 - c}, device_id_type=MESH)
    pl.semaphore_wait(barrier, n + 2)

    def remote(src, dst, send, recv, **device):
        return pltpu.make_async_remote_copy(
            src_ref=src, dst_ref=dst, send_sem=send, recv_sem=recv, device_id=device, device_id_type=MESH
        )

    def w_rows(owner, which, q):
        return pl.ds(pl.multiple_of(owner * depth + which * half + q * piece, piece), piece)

    def w_pack(j, i):
        dest = lax.rem(s + j, n)
        return pltpu.make_async_copy(
            weights[i].at[pl.ds(pl.multiple_of(g * half, half), half), pl.ds(pl.multiple_of(dest * HD, HD), HD)],
            packed.at[j - 1, :, pl.ds(i * HD, HD)], pack_sem.at[j - 1, i],
        )

    def w_copy(j, q):
        return remote(
            packed.at[j - 1, pl.ds(q * piece, piece), :], w_all.at[w_rows(s, g, q), :],
            w_send.at[j - 1, q], w_recv.at[j - 1, q], seq=lax.rem(s + j, n),
        )

    def w_arrival(j, q):
        here = w_all.at[w_rows(lax.rem(s + n - j, n), g, q), :]
        return remote(here, here, w_send.at[j - 1, q], w_recv.at[j - 1, q], seq=lax.rem(s + j, n))

    def y_copy(j, q, which=g):
        here = w_all.at[w_rows(lax.rem(s + n - j, n), which, q), :]
        return remote(here, here, y_send.at[j - 1, q], y_recv.at[j - 1, q], groups=1 - g)

    def y_arrival(j, q):
        return y_copy(j, q, 1 - g)

    def spot(b, rr, cc, k):
        return x_all.at[b, cc, pl.ds(pl.multiple_of(rr * rows + k * part, part), part), :]

    def source(b, k, own):
        return acts.at[pl.ds(pl.multiple_of(k * part, part), part), :] if own else spot(b, r, c, k)

    def up_copy(b, k, own=False):
        return remote(source(b, k, own), spot(b, r, c, k), up_send.at[b, k], z_recv.at[b, k], seq=s + 1)

    def down_copy(b, k, own=False):
        return remote(source(b, k, own), spot(b, r, c, k), down_send.at[b, k], z_recv.at[b, k], seq=s - 1)

    def x_copy(b, k, own=False):
        return remote(source(b, k, own), spot(b, r, c, k), x_send.at[b, k], x_recv.at[b, k], row=1 - r)

    def x_arrival(b, k):
        here = spot(b, 1 - r, c, k)
        return remote(here, here, x_send.at[b, k], x_recv.at[b, k], row=1 - r)

    def c_copy(b, k, rr, own=False):
        src = source(b, k, True) if own else spot(b, rr, c, k)
        return remote(src, spot(b, rr, c, k), c_send.at[rr, b, k], c_recv.at[rr, b, k], col=1 - c)

    def c_arrival(b, k, rr):
        here = spot(b, rr, 1 - c, k)
        return remote(here, here, c_send.at[rr, b, k], c_recv.at[rr, b, k], col=1 - c)

    for j in range(1, n):
        for i in range(3):
            w_pack(j, i).start()
    for j in range(1, n):
        for i in range(3):
            w_pack(j, i).wait()
        for q in range(PIECES):
            w_copy(j, q).start()

    @pl.loop(0, CHUNKS)
    def _(k):
        @pl.when(s < n - 1)
        def _():
            up_copy(s, k, True).start()

        @pl.when(s > 0)
        def _():
            down_copy(s, k, True).start()

        x_copy(s, k, True).start()
        c_copy(s, k, r, True).start()

    own_copies = [
        pltpu.make_async_copy(
            acts, x_all.at[s, c, pl.ds(pl.multiple_of(r * rows, rows), rows), :], local_sem.at[0]
        )
    ] + [
        pltpu.make_async_copy(
            weights[i].at[:, pl.ds(pl.multiple_of(s * HD, HD), HD)],
            w_all.at[pl.ds(pl.multiple_of(s * depth, depth), depth), pl.ds(i * HD, HD)],
            local_sem.at[1 + i],
        )
        for i in range(3)
    ]
    for copy in own_copies:
        copy.start()

    def each_at(t, body):
        if t == 0:
            body(s, 0)
            return
        pl.when(s - t >= 0)(lambda: body(s - t, 1))
        pl.when(s + t < n)(lambda: body(s + t, -1))

    def pass_on(b, side, k):
        here = spot(b, r, c, k)
        remote(here, here, up_send.at[b, k], z_recv.at[b, k], row=1 - r).wait_recv()
        if side > 0:
            pl.when(s < n - 1)(lambda: up_copy(b, k).start())
        else:
            pl.when(s > 0)(lambda: down_copy(b, k).start())
        x_copy(b, k).start()
        c_copy(b, k, r).start()

    def across(b, k):
        x_arrival(b, k).wait_recv()
        c_copy(b, k, 1 - r).start()

    def project(t):
        @pl.loop(0, 2 if t else 1)
        def _(side):
            b = s + (2 * side - 1) * t

            @pl.when((b >= 0) & (b < n))
            def _():
                @pl.loop(0, CHUNKS)
                def _(k):
                    c_arrival(b, k, 0).wait_recv()
                    c_arrival(b, k, 1).wait_recv()

                total = jnp.dot(x_all[b, 0], w_all[:half_width, :], preferred_element_type=jnp.float32)
                total += jnp.dot(x_all[b, 1], w_all[half_width:, :], preferred_element_type=jnp.float32)
                qkv[pl.ds(pl.multiple_of(b * block, block), block), :] = total.astype(jnp.bfloat16)

    for t in range(1, n):
        for k in range(CHUNKS):
            each_at(t, lambda b, side: pass_on(b, side, k))
            each_at(t - 1, lambda b, side: across(b, k))
            if t == 1 and 1 <= k <= PIECES:
                for j in range(1, n):
                    w_arrival(j, k - 1).wait_recv()
                    y_copy(j, k - 1).start()
            if t == n - 1 and k == 0:
                for copy in own_copies:
                    copy.wait()
                for j in range(1, n):
                    for q in range(PIECES):
                        y_arrival(j, q).wait_recv()
            if t == n - 1 and k < n - 2:
                project(k)
    project(n - 2)

    @pl.loop(0, CHUNKS)
    def _(k):
        each_at(n - 1, lambda b, side: across(b, k))

    project(n - 1)

    rate = math.log2(math.e) / math.sqrt(HD)

    def o_copy(j):
        dest = lax.rem(s + j, n)
        return remote(
            heads_out.at[dest], out.at[:, pl.ds(pl.multiple_of(s * HD, HD), HD)],
            o_send.at[j - 1], o_recv.at[j - 1], seq=dest,
        )

    def o_arrival(j):
        owner = lax.rem(s + n - j, n)
        here = out.at[:, pl.ds(pl.multiple_of(owner * HD, HD), HD)]
        return remote(heads_out.at[owner], here, o_send.at[j - 1], o_recv.at[j - 1], seq=owner)

    @pl.loop(1, n + 1)
    def _(j):
        b = lax.rem(s + j, n)
        query = qkv[pl.ds(pl.multiple_of(b * block, block), block), pl.ds(0, HD)]
        keys = qkv[:, pl.ds(HD, HD)]
        values = qkv[:, pl.ds(2 * HD, HD)]
        scores = lax.dot_general(
            query, keys, (((1,), (1,)), ((), ())), preferred_element_type=jnp.float32
        )
        expos = jnp.exp2((scores - jnp.max(scores, axis=-1, keepdims=True)) * rate)
        total = jnp.sum(expos, axis=-1, keepdims=True)
        summed = jnp.dot(expos.astype(jnp.bfloat16), values, preferred_element_type=jnp.float32)
        heads_out[b] = (summed / total).astype(jnp.bfloat16)
        pl.when(j < n)(lambda: o_copy(j).start())

    own_out = pltpu.make_async_copy(
        heads_out.at[s], out.at[:, pl.ds(pl.multiple_of(s * HD, HD), HD)], local_sem.at[0]
    )
    own_out.start()

    for j in range(1, n):
        for q in range(PIECES):
            w_copy(j, q).wait_send()
            y_copy(j, q).wait_send()

    @pl.loop(0, n)
    def _(b):
        @pl.loop(0, CHUNKS)
        def _(k):
            pl.when((s < n - 1) & (b <= s))(lambda: up_copy(b, k).wait_send())
            pl.when((s > 0) & (b >= s))(lambda: down_copy(b, k).wait_send())
            x_copy(b, k).wait_send()
            c_copy(b, k, 0).wait_send()
            c_copy(b, k, 1).wait_send()

    own_out.wait()
    for j in range(1, n):
        o_copy(j).wait_send()
        o_arrival(j).wait_recv()


def one_head_per_device(acts, w_query, w_key, w_value):
    n = lax.axis_size("seq")
    rows, half_width = acts.shape
    depth, width = w_query.shape
    tokens = n * 2 * rows
    dma = pltpu.SemaphoreType.DMA
    flops = 2 * tokens * depth * n * 3 * HD + 4 * tokens * tokens * HD
    return pl.pallas_call(
        functools.partial(head_kernel, n),
        out_shape=jax.ShapeDtypeStruct((2 * rows, width), jnp.bfloat16),
        in_specs=[pl.BlockSpec(memory_space=pl.ANY)] * 4,
        out_specs=pl.BlockSpec(memory_space=pl.ANY),
        scratch_shapes=[
            pltpu.VMEM((n, 2, 2 * rows, half_width), jnp.bfloat16),
            pltpu.VMEM((n * depth, 3 * HD), jnp.bfloat16),
            pltpu.VMEM((n - 1, depth // 2, 3 * HD), jnp.bfloat16),
            pltpu.VMEM((tokens, 3 * HD), jnp.bfloat16),
            pltpu.VMEM((n, 2 * rows, HD), jnp.bfloat16),
            dma((4,)), dma((n - 1, 3)),
            dma((n - 1, PIECES)), dma((n - 1, PIECES)), dma((n - 1, PIECES)), dma((n - 1, PIECES)),
            dma((n, CHUNKS)), dma((n, CHUNKS)), dma((n, CHUNKS)),
            dma((n, CHUNKS)), dma((n, CHUNKS)),
            dma((2, n, CHUNKS)), dma((2, n, CHUNKS)),
            dma((n - 1,)), dma((n - 1,)),
        ],
        compiler_params=pltpu.CompilerParams(
            collective_id=0, has_side_effects=True, vmem_limit_bytes=63 * 1024 * 1024
        ),
        cost_estimate=pl.CostEstimate(flops=flops, bytes_accessed=2 * tokens * half_width, transcendentals=tokens * tokens),
    )(acts, w_query, w_key, w_value)


def passed_along(block, axis, distance):
    devices = range(lax.axis_size(axis))
    route = [((i - distance) % len(devices), i) for i in devices]
    return lax.ppermute(block, axis, route)


def blocks_passed_along(acts, w_query, w_key, w_value):
    block = lax.all_gather(acts, "row", axis=0, tiled=True)
    block = lax.all_gather(block, "col", axis=1, tiled=True)
    tokens_here = block.shape[0]
    width = w_query.shape[1]
    heads_here = width // HD
    pieces = (
        lax.all_gather(w_query, "seq", axis=0, tiled=True),
        lax.all_gather(w_key, "seq", axis=0, tiled=True),
        lax.all_gather(w_value, "seq", axis=0, tiled=True),
    )
    query_sum, key_sum, value_sum = tuple(
        (jnp.dot(block, piece, preferred_element_type=jnp.float32) for piece in pieces)
    )
    query = query_sum.astype(jnp.bfloat16).reshape(tokens_here, heads_here, HD)
    packed = jnp.stack([key_sum.astype(jnp.bfloat16), value_sum.astype(jnp.bfloat16)])
    blocks_seen = [packed]
    current = packed
    for step in range(1, SPAN):
        current = passed_along(current, "seq", 1)
        blocks_seen.append(current)
    scale = 1.0 / jnp.sqrt(jnp.float32(HD))
    score_list = []
    for seen in blocks_seen:
        seen_keys = seen[0].reshape(-1, heads_here, HD)
        score_list.append(
            jnp.einsum("qhd,khd->hqk", query, seen_keys, preferred_element_type=jnp.float32) * scale
        )
    largest = score_list[0].max(axis=-1, keepdims=True)
    for scores in score_list[1:]:
        largest = jnp.maximum(largest, scores.max(axis=-1, keepdims=True))
    running_total = jnp.zeros((heads_here, tokens_here), jnp.float32)
    summed = jnp.zeros((tokens_here, heads_here, HD), jnp.float32)
    for scores, seen in zip(score_list, blocks_seen):
        expos = jnp.exp(scores - largest)
        running_total = running_total + jnp.sum(expos, axis=-1)
        seen_values = seen[1].reshape(-1, heads_here, HD)
        summed = summed + jnp.einsum(
            "hqk,khd->qhd",
            expos.astype(jnp.bfloat16),
            seen_values,
            preferred_element_type=jnp.float32,
        )
    attended = summed / jnp.transpose(running_total)[:, :, None]
    return attended.astype(jnp.bfloat16).reshape(tokens_here, width)


def per_device(acts, w_query, w_key, w_value):
    n = lax.axis_size("seq")
    pairs = all(lax.axis_size(axis) == 2 for axis in ("groups", "row", "col"))
    depth, width = w_query.shape
    if pairs and n == SPAN and width == n * HD and acts.shape[0] % (16 * CHUNKS) == 0 and depth % (32 * PIECES) == 0:
        return one_head_per_device(acts, w_query, w_key, w_value)
    return blocks_passed_along(acts, w_query, w_key, w_value)


def solution(mesh):
    in_specs = (
        P(("groups", "seq", "row"), "col"),
        P("seq", ("row", "col")),
        P("seq", ("row", "col")),
        P("seq", ("row", "col")),
    )
    out_specs = P(("groups", "seq"), ("row", "col"))
    return jax.shard_map(
        per_device, mesh=mesh, in_specs=in_specs, out_specs=out_specs, check_vma=False
    )
```

```python
import functools
import math

import jax
import jax.numpy as jnp
from jax import lax
from jax.experimental import pallas as pl
from jax.experimental.pallas import tpu as pltpu
from jax.sharding import PartitionSpec as P

HD = 128
SPAN = 4
CHUNKS = 6
MESH = pl.DeviceIdType.MESH


def head_kernel(
    n, acts, w_query, w_key, w_value, out,
    x_all, w_all, qkv, heads_out, tops, totals, sums,
    local_sem, w_send, w_recv, y_send, y_recv,
    up_send, down_send, z_recv, x_send, x_recv, c_send, c_recv, o_send, o_recv,
):
    g, s = lax.axis_index("groups"), lax.axis_index("seq")
    r, c = lax.axis_index("row"), lax.axis_index("col")
    weights = (w_query, w_key, w_value)
    rows, half_width = acts.shape
    depth = w_query.shape[0]
    half = depth // 2
    block = 2 * rows
    part = rows // CHUNKS

    barrier = pltpu.get_barrier_semaphore()
    for j in range(1, n):
        pl.semaphore_signal(barrier, inc=1, device_id={"seq": lax.rem(s + j, n)}, device_id_type=MESH)
    pl.semaphore_signal(barrier, inc=1, device_id={"groups": 1 - g}, device_id_type=MESH)
    pl.semaphore_signal(barrier, inc=1, device_id={"row": 1 - r}, device_id_type=MESH)
    pl.semaphore_signal(barrier, inc=1, device_id={"col": 1 - c}, device_id_type=MESH)
    pl.semaphore_wait(barrier, n + 2)

    def remote(src, dst, send, recv, **device):
        return pltpu.make_async_remote_copy(
            src_ref=src, dst_ref=dst, send_sem=send, recv_sem=recv, device_id=device, device_id_type=MESH
        )

    def w_rows(owner, which):
        return pl.ds(pl.multiple_of(owner * depth + which * half, half), half)

    def w_copy(j, i):
        dest = lax.rem(s + j, n)
        return remote(
            weights[i].at[pl.ds(pl.multiple_of(g * half, half), half), pl.ds(pl.multiple_of(dest * HD, HD), HD)],
            w_all.at[w_rows(s, g), pl.ds(i * HD, HD)],
            w_send.at[j - 1, i], w_recv.at[j - 1, i], seq=dest,
        )

    def w_arrival(j, i):
        owner = lax.rem(s + n - j, n)
        here = w_all.at[w_rows(owner, g), pl.ds(i * HD, HD)]
        return remote(here, here, w_send.at[j - 1, i], w_recv.at[j - 1, i], seq=lax.rem(s + j, n))

    def y_copy(j, i, which=g):
        owner = lax.rem(s + n - j, n)
        here = w_all.at[w_rows(owner, which), pl.ds(i * HD, HD)]
        return remote(here, here, y_send.at[j - 1, i], y_recv.at[j - 1, i], groups=1 - g)

    def y_arrival(j, i):
        return y_copy(j, i, 1 - g)

    def spot(b, rr, cc, k):
        return x_all.at[b, cc, pl.ds(pl.multiple_of(rr * rows + k * part, part), part), :]

    def source(b, k, own):
        return acts.at[pl.ds(pl.multiple_of(k * part, part), part), :] if own else spot(b, r, c, k)

    def up_copy(b, k, own=False):
        return remote(source(b, k, own), spot(b, r, c, k), up_send.at[b, k], z_recv.at[b, k], seq=s + 1)

    def down_copy(b, k, own=False):
        return remote(source(b, k, own), spot(b, r, c, k), down_send.at[b, k], z_recv.at[b, k], seq=s - 1)

    def x_copy(b, k, own=False):
        return remote(source(b, k, own), spot(b, r, c, k), x_send.at[b, k], x_recv.at[b, k], row=1 - r)

    def x_arrival(b, k):
        here = spot(b, 1 - r, c, k)
        return remote(here, here, x_send.at[b, k], x_recv.at[b, k], row=1 - r)

    def c_copy(b, k, rr, own=False):
        src = source(b, k, True) if own else spot(b, rr, c, k)
        return remote(src, spot(b, rr, c, k), c_send.at[rr, b, k], c_recv.at[rr, b, k], col=1 - c)

    def c_arrival(b, k, rr):
        here = spot(b, rr, 1 - c, k)
        return remote(here, here, c_send.at[rr, b, k], c_recv.at[rr, b, k], col=1 - c)

    for i in range(3):
        for j in range(1, n):
            w_copy(j, i).start()

    @pl.loop(0, CHUNKS)
    def _(k):
        @pl.when(s < n - 1)
        def _():
            up_copy(s, k, True).start()

        @pl.when(s > 0)
        def _():
            down_copy(s, k, True).start()

        x_copy(s, k, True).start()
        c_copy(s, k, r, True).start()

    own_copies = [
        pltpu.make_async_copy(
            acts, x_all.at[s, c, pl.ds(pl.multiple_of(r * rows, rows), rows), :], local_sem.at[0]
        )
    ] + [
        pltpu.make_async_copy(
            weights[i].at[:, pl.ds(pl.multiple_of(s * HD, HD), HD)],
            w_all.at[pl.ds(pl.multiple_of(s * depth, depth), depth), pl.ds(i * HD, HD)],
            local_sem.at[1 + i],
        )
        for i in range(3)
    ]
    for copy in own_copies:
        copy.start()

    def each_at(t, body):
        if t == 0:
            body(s, 0)
            return
        pl.when(s - t >= 0)(lambda: body(s - t, 1))
        pl.when(s + t < n)(lambda: body(s + t, -1))

    def pass_on(b, side, k):
        here = spot(b, r, c, k)
        remote(here, here, up_send.at[b, k], z_recv.at[b, k], row=1 - r).wait_recv()
        if side > 0:
            pl.when(s < n - 1)(lambda: up_copy(b, k).start())
        else:
            pl.when(s > 0)(lambda: down_copy(b, k).start())
        x_copy(b, k).start()
        c_copy(b, k, r).start()

    def across(b, k):
        x_arrival(b, k).wait_recv()
        c_copy(b, k, 1 - r).start()

    def project(t):
        @pl.loop(0, 2 if t else 1)
        def _(side):
            b = s + (2 * side - 1) * t

            @pl.when((b >= 0) & (b < n))
            def _():
                @pl.loop(0, CHUNKS)
                def _(k):
                    c_arrival(b, k, 0).wait_recv()
                    c_arrival(b, k, 1).wait_recv()

                total = jnp.dot(x_all[b, 0], w_all[:half_width, :], preferred_element_type=jnp.float32)
                total += jnp.dot(x_all[b, 1], w_all[half_width:, :], preferred_element_type=jnp.float32)
                qkv[pl.ds(pl.multiple_of(b * block, block), block), :] = total.astype(jnp.bfloat16)

    rate = math.log2(math.e) / math.sqrt(HD)
    at_end = (s == 0) | (s == n - 1)
    far = n - 1 - s

    def of_block(b, what):
        return qkv[pl.ds(pl.multiple_of(b * block, block), block), pl.ds(what * HD, HD)]

    def scores_of(query, keys):
        return lax.dot_general(query, keys, (((1,), (1,)), ((), ())), preferred_element_type=jnp.float32)

    def weigh(scores, top, values):
        expos = jnp.exp2((scores - top) * rate)
        summed = jnp.dot(expos.astype(jnp.bfloat16), values, preferred_element_type=jnp.float32)
        return jnp.sum(expos, axis=-1, keepdims=True), summed

    def attend_near(i):
        @pl.when(at_end)
        def _():
            b = jnp.where(s == 0, i, n - 1 - i)
            near = pl.ds(pl.multiple_of(jnp.where(s == 0, 0, block), block), (n - 1) * block)
            scores = scores_of(of_block(b, 0), qkv[near, pl.ds(HD, HD)])
            top = jnp.max(scores, axis=-1, keepdims=True)
            tops[b] = top
            totals[b], sums[b] = weigh(scores, top, qkv[near, pl.ds(2 * HD, HD)])

    for t in range(1, n):
        for k in range(CHUNKS):
            each_at(t, lambda b, side: pass_on(b, side, k))
            each_at(t - 1, lambda b, side: across(b, k))
            if t == 1 and 1 <= k <= 3:
                for j in range(1, n):
                    w_arrival(j, k - 1).wait_recv()
                    y_copy(j, k - 1).start()
            if t == n - 1 and k == 0:
                for copy in own_copies:
                    copy.wait()
                for j in range(1, n):
                    for i in range(3):
                        y_arrival(j, i).wait_recv()
            if t == n - 1 and k < n - 2:
                project(k)
    project(n - 2)

    for k in range(CHUNKS):
        each_at(n - 1, lambda b, side: across(b, k))
        if CHUNKS - n <= k < CHUNKS - 1:
            attend_near(k - (CHUNKS - n))

    project(n - 1)

    def o_copy(b):
        j = lax.rem(b - s + n, n)
        return remote(
            heads_out.at[b], out.at[:, pl.ds(pl.multiple_of(s * HD, HD), HD)],
            o_send.at[j - 1], o_recv.at[j - 1], seq=b,
        )

    def o_arrival(j):
        owner = lax.rem(s + n - j, n)
        here = out.at[:, pl.ds(pl.multiple_of(owner * HD, HD), HD)]
        return remote(heads_out.at[owner], here, o_send.at[j - 1], o_recv.at[j - 1], seq=owner)

    def give(b, summed, total):
        heads_out[b] = (summed / total).astype(jnp.bfloat16)
        pl.when(b != s)(lambda: o_copy(b).start())

    @pl.loop(1, jnp.where(at_end, 2, n + 1))
    def _(j):
        b = jnp.where(at_end, far, lax.rem(s + j, n))
        scores = scores_of(of_block(b, 0), qkv[:, pl.ds(HD, HD)])
        top = jnp.max(scores, axis=-1, keepdims=True)
        total, summed = weigh(scores, top, qkv[:, pl.ds(2 * HD, HD)])
        give(b, summed, total)

    @pl.when(at_end)
    def _():
        @pl.loop(0, n - 1)
        def _(i):
            b = jnp.where(s == 0, n - 2 - i, 1 + i)
            scores = scores_of(of_block(b, 0), of_block(far, 1))
            top = jnp.maximum(tops[b], jnp.max(scores, axis=-1, keepdims=True))
            total, summed = weigh(scores, top, of_block(far, 2))
            shrink = jnp.exp2((tops[b] - top) * rate)
            give(b, sums[b] * shrink + summed, totals[b] * shrink + total)

    own_out = pltpu.make_async_copy(
        heads_out.at[s], out.at[:, pl.ds(pl.multiple_of(s * HD, HD), HD)], local_sem.at[0]
    )
    own_out.start()

    for j in range(1, n):
        for i in range(3):
            w_copy(j, i).wait_send()
            y_copy(j, i).wait_send()

    @pl.loop(0, n)
    def _(b):
        @pl.loop(0, CHUNKS)
        def _(k):
            pl.when((s < n - 1) & (b <= s))(lambda: up_copy(b, k).wait_send())
            pl.when((s > 0) & (b >= s))(lambda: down_copy(b, k).wait_send())
            x_copy(b, k).wait_send()
            c_copy(b, k, 0).wait_send()
            c_copy(b, k, 1).wait_send()

    own_out.wait()
    for j in range(1, n):
        o_copy(lax.rem(s + j, n)).wait_send()
        o_arrival(j).wait_recv()


def one_head_per_device(acts, w_query, w_key, w_value):
    n = lax.axis_size("seq")
    rows, half_width = acts.shape
    depth, width = w_query.shape
    tokens = n * 2 * rows
    dma = pltpu.SemaphoreType.DMA
    flops = 2 * tokens * depth * n * 3 * HD + 4 * tokens * tokens * HD
    return pl.pallas_call(
        functools.partial(head_kernel, n),
        out_shape=jax.ShapeDtypeStruct((2 * rows, width), jnp.bfloat16),
        in_specs=[pl.BlockSpec(memory_space=pl.ANY)] * 4,
        out_specs=pl.BlockSpec(memory_space=pl.ANY),
        scratch_shapes=[
            pltpu.VMEM((n, 2, 2 * rows, half_width), jnp.bfloat16),
            pltpu.VMEM((n * depth, 3 * HD), jnp.bfloat16),
            pltpu.VMEM((tokens, 3 * HD), jnp.bfloat16),
            pltpu.VMEM((n, 2 * rows, HD), jnp.bfloat16),
            pltpu.VMEM((n, 2 * rows, 1), jnp.float32),
            pltpu.VMEM((n, 2 * rows, 1), jnp.float32),
            pltpu.VMEM((n, 2 * rows, HD), jnp.float32),
            dma((4,)),
            dma((n - 1, 3)), dma((n - 1, 3)), dma((n - 1, 3)), dma((n - 1, 3)),
            dma((n, CHUNKS)), dma((n, CHUNKS)), dma((n, CHUNKS)),
            dma((n, CHUNKS)), dma((n, CHUNKS)),
            dma((2, n, CHUNKS)), dma((2, n, CHUNKS)),
            dma((n - 1,)), dma((n - 1,)),
        ],
        compiler_params=pltpu.CompilerParams(
            collective_id=0, has_side_effects=True, vmem_limit_bytes=63 * 1024 * 1024
        ),
        cost_estimate=pl.CostEstimate(flops=flops, bytes_accessed=2 * tokens * half_width, transcendentals=tokens * tokens),
    )(acts, w_query, w_key, w_value)


def passed_along(block, axis, distance):
    devices = range(lax.axis_size(axis))
    route = [((i - distance) % len(devices), i) for i in devices]
    return lax.ppermute(block, axis, route)


def blocks_passed_along(acts, w_query, w_key, w_value):
    block = lax.all_gather(acts, "row", axis=0, tiled=True)
    block = lax.all_gather(block, "col", axis=1, tiled=True)
    tokens_here = block.shape[0]
    width = w_query.shape[1]
    heads_here = width // HD
    pieces = (
        lax.all_gather(w_query, "seq", axis=0, tiled=True),
        lax.all_gather(w_key, "seq", axis=0, tiled=True),
        lax.all_gather(w_value, "seq", axis=0, tiled=True),
    )
    query_sum, key_sum, value_sum = tuple(
        (jnp.dot(block, piece, preferred_element_type=jnp.float32) for piece in pieces)
    )
    query = query_sum.astype(jnp.bfloat16).reshape(tokens_here, heads_here, HD)
    packed = jnp.stack([key_sum.astype(jnp.bfloat16), value_sum.astype(jnp.bfloat16)])
    blocks_seen = [packed]
    current = packed
    for step in range(1, SPAN):
        current = passed_along(current, "seq", 1)
        blocks_seen.append(current)
    scale = 1.0 / jnp.sqrt(jnp.float32(HD))
    score_list = []
    for seen in blocks_seen:
        seen_keys = seen[0].reshape(-1, heads_here, HD)
        score_list.append(
            jnp.einsum("qhd,khd->hqk", query, seen_keys, preferred_element_type=jnp.float32) * scale
        )
    largest = score_list[0].max(axis=-1, keepdims=True)
    for scores in score_list[1:]:
        largest = jnp.maximum(largest, scores.max(axis=-1, keepdims=True))
    running_total = jnp.zeros((heads_here, tokens_here), jnp.float32)
    summed = jnp.zeros((tokens_here, heads_here, HD), jnp.float32)
    for scores, seen in zip(score_list, blocks_seen):
        expos = jnp.exp(scores - largest)
        running_total = running_total + jnp.sum(expos, axis=-1)
        seen_values = seen[1].reshape(-1, heads_here, HD)
        summed = summed + jnp.einsum(
            "hqk,khd->qhd",
            expos.astype(jnp.bfloat16),
            seen_values,
            preferred_element_type=jnp.float32,
        )
    attended = summed / jnp.transpose(running_total)[:, :, None]
    return attended.astype(jnp.bfloat16).reshape(tokens_here, width)


def per_device(acts, w_query, w_key, w_value):
    n = lax.axis_size("seq")
    pairs = all(lax.axis_size(axis) == 2 for axis in ("groups", "row", "col"))
    depth, width = w_query.shape
    if pairs and n == SPAN and width == n * HD and acts.shape[0] % (16 * CHUNKS) == 0 and depth % 32 == 0:
        return one_head_per_device(acts, w_query, w_key, w_value)
    return blocks_passed_along(acts, w_query, w_key, w_value)


def solution(mesh):
    in_specs = (
        P(("groups", "seq", "row"), "col"),
        P("seq", ("row", "col")),
        P("seq", ("row", "col")),
        P("seq", ("row", "col")),
    )
    out_specs = P(("groups", "seq"), ("row", "col"))
    return jax.shard_map(
        per_device, mesh=mesh, in_specs=in_specs, out_specs=out_specs, check_vma=False
    )
```
